256 devices in a mesh: front: 2 (over y_lo), row: 8 (over y_hi, x), col: 16 (over z, core).
Axes of the slice: x: 4, y: 4 (y_hi: 2, y_lo: 2; y = y_hi * 2 + y_lo), z: 8, core: 2. Of those that a mesh axis runs over, the one named last changes fastest.
Arguments:
- front_orig: bfloat16 [2, 12288, 12288], P('front', 'row', 'col'), as said below
- child_update: bfloat16 [8192, 32768], P(('front', 'row'), 'col'), as said below
- tile_map: int32 [2, 2, 64], replicated, may hold values from 0 to 95, as said below
Outputs:
- update: float32 [2, 12288, 12288], P('front', 'row', 'col')
- factor: float32 [2, 12288, 512], P('front', 'row')
The draws below stay inside these ranges and needn't reach their ends.
Inputs may be any that keep to these rules, and one draw needn't show every extreme that they name: For every f and c, tile_map[f, c] is one-to-one. tile_map[f, c, i] mod 16 depends only on i mod 16 and takes each of its 16 values once over 16 consecutive i; tile_map[f, c, i] mod 8 depends only on i mod 8. `front_orig`: each front is symmetric in logical order. `child_update`: each child's 8192 x 8192 matrix is symmetric.
All inputs are finite; a program needn't handle non-finite values.
Results may differ from the reference program's by a relative error of at most 0.0009.
Values may be sent and summed in bfloat16 or wider, within the bound.
No kernel may reach another device: no remote copies, remote signals or barrier semaphores. Data moves between devices by JAX's collectives and lax.ppermute only.
A program may use at most 128 MiB of HBM per device.

```python
import math
import jax
import jax.numpy as jnp
from jax import lax

TILE = 128
NF = 12288
NC = 8192
PANELS = 2
PANEL = 256
NT = 96
NCT = 64
N_ROW = 8
N_COL = 16


def symmetric_noise(key, count, order):
    raw_draw = jax.random.normal(key, (count, order, order), jnp.float32)
    return (raw_draw + jnp.swapaxes(raw_draw, 1, 2)) * 0.70710678


def to_storage(matrix):
    shaped = matrix.reshape(2, NT // N_ROW, N_ROW, TILE, NF).transpose(0, 2, 1, 3, 4).reshape(2, NF, NF)
    shaped = shaped.reshape(2, NF, NT // N_COL, N_COL, TILE).transpose(0, 1, 3, 2, 4).reshape(2, NF, NF)
    return shaped


def draw_front_orig(key, part):
    key_noise, key_diag, key_rank = jax.random.split(key, 3)
    matrix = symmetric_noise(key_noise, 2, NF) * (0.25 / math.sqrt(NF))
    diag_vals = jax.random.uniform(key_diag, (2, NF), jnp.float32, 2.5, 3.5)
    factor_vals = jax.random.normal(key_rank, (4, 2, NF), jnp.float32) * 0.125
    for factor_no in range(4):
        matrix = matrix + factor_vals[factor_no][:, :, None] * factor_vals[factor_no][:, None, :]
    identity = jnp.eye(NF, dtype=jnp.float32)
    matrix = matrix + diag_vals[:, :, None] * identity[None]
    return to_storage(matrix).astype(jnp.bfloat16)


def draw_child_update(key, part):
    key_noise, key_diag = jax.random.split(key, 2)
    matrix = symmetric_noise(key_noise, 4, NC) * (0.25 / math.sqrt(NC))
    shrink = jax.random.uniform(key_diag, (4, NC), jnp.float32, 0.125, 0.375)
    identity = jnp.eye(NC, dtype=jnp.float32)
    matrix = matrix - shrink[:, :, None] * identity[None]
    return matrix.transpose(1, 0, 2).reshape(NC, 4 * NC).astype(jnp.bfloat16)


def pick_quotients(key):
    per_class = NCT // N_COL
    quotients = NT // N_COL
    key_mid, key_order = jax.random.split(key, 2)
    middle = 1 + jax.random.permutation(key_mid, quotients - 2)[:per_class - 2]
    chosen = jnp.concatenate([jnp.array([0, quotients - 1], dtype=jnp.int32), middle.astype(jnp.int32)])
    return chosen[jax.random.permutation(key_order, per_class)]


def one_map(key):
    key_rho, key_high, key_quot = jax.random.split(key, 3)
    rho_perm = jax.random.permutation(key_rho, N_ROW).astype(jnp.int32)
    high_perm = jax.random.permutation(key_high, N_COL // N_ROW).astype(jnp.int32)
    residue_ids = jnp.arange(N_COL)
    residues = rho_perm[residue_ids % N_ROW] + N_ROW * high_perm[residue_ids // N_ROW]
    quot_table = jax.vmap(pick_quotients)(jax.random.split(key_quot, N_COL))
    child_ids = jnp.arange(NCT)
    return N_COL * quot_table[child_ids % N_COL, child_ids // N_COL] + residues[child_ids % N_COL]


def draw_tile_map(key, part):
    key_list = jax.random.split(jax.random.fold_in(key, 7), 4)
    return jax.vmap(one_map)(key_list).reshape(2, 2, NCT).astype(jnp.int32)


def setup_inputs(seed: int = 0) -> dict:
    splits = jax.random.split(jax.random.key(seed), 4)
    front_orig = draw_front_orig(jax.random.fold_in(splits[3], 71), 0)
    child_update = draw_child_update(jax.random.fold_in(splits[3], 71), 0)
    tile_map = draw_tile_map(jax.random.fold_in(splits[3], 71), 0)
    return dict(front_orig=front_orig, child_update=child_update, tile_map=tile_map)


def reorder_rows(matrix, groups, forward):
    per_group = matrix.shape[0] // TILE // groups
    if forward:
        shaped = matrix.reshape(groups, per_group, TILE, matrix.shape[1])
    else:
        shaped = matrix.reshape(per_group, groups, TILE, matrix.shape[1])
    return shaped.transpose(1, 0, 2, 3).reshape(matrix.shape)

def reference(front_orig, child_update, tile_map):
    identity = jnp.eye(PANEL, dtype=jnp.float32)
    row_index = jnp.arange(NF)
    updates = []
    factors = []
    for parent in range(2):
        front_mat = front_orig[parent].astype(jnp.float32)
        front_mat = reorder_rows(front_mat, N_ROW, True)
        front_mat = reorder_rows(front_mat.T, N_COL, True).T
        tile_grid = front_mat.reshape(NT, TILE, NT, TILE).transpose(0, 2, 1, 3)
        for sibling in range(2):
            column_start = (2 * parent + sibling) * NC
            child_mat = child_update[:, column_start:column_start + NC].astype(jnp.float32)
            child_grid = child_mat.reshape(NCT, TILE, NCT, TILE).transpose(0, 2, 1, 3)
            mapped = tile_map[parent, sibling]
            tile_grid = tile_grid.at[mapped[:, None], mapped[None, :]].add(child_grid)
        front_mat = tile_grid.transpose(0, 2, 1, 3).reshape(NF, NF)
        columns = []
        for panel_no in range(PANELS):
            start_col = panel_no * PANEL
            stop_col = start_col + PANEL
            lower_f = jnp.linalg.cholesky(front_mat[start_col:stop_col, start_col:stop_col])
            inverse = jax.scipy.linalg.solve_triangular(lower_f, identity, lower=True)
            panel_cols = jnp.dot(front_mat[:, start_col:stop_col].astype(jnp.float32), inverse.T.astype(jnp.float32), precision=lax.Precision.HIGHEST, preferred_element_type=jnp.float32)
            panel_cols = jnp.where((row_index >= start_col)[:, None], panel_cols, 0.0)
            columns.append(panel_cols)
            trail_rows = jnp.where((row_index >= stop_col)[:, None], panel_cols, 0.0)
            front_mat = front_mat - jnp.dot(trail_rows.astype(jnp.float32), trail_rows.T.astype(jnp.float32), precision=lax.Precision.HIGHEST, preferred_element_type=jnp.float32)
        front_mat = reorder_rows(front_mat, N_ROW, False)
        front_mat = reorder_rows(front_mat.T, N_COL, False).T
        updates.append(front_mat)
        factors.append(reorder_rows(jnp.concatenate(columns, axis=1), N_ROW, False))
    return (jnp.stack(updates), jnp.stack(factors))
```

```python
import functools

import jax
import jax.numpy as jnp
from jax import lax
from jax.experimental import pallas as pl
from jax.experimental.pallas import tpu as pltpu
from jax.sharding import Mesh
from jax.sharding import PartitionSpec as P

TILE = 128
PANEL = 256
KDIM = 512
NT = 96
NCT = 64
ROW = ("rowh", "xlo")
COL = ("z", "core")
PIECE = 8
F32 = jnp.float32
BF16 = jnp.bfloat16
HIGHEST = lax.Precision.HIGHEST


def pack_first(index, child):
    def body(index_ref, child_ref, out_ref):
        for a in range(4):
            for b in range(16):
                tile = child_ref[a * TILE : (a + 1) * TILE, b * TILE : (b + 1) * TILE]
                out_ref[index_ref[a * 16 + b]] = tile

    return pl.pallas_call(
        body,
        out_shape=jax.ShapeDtypeStruct((64, TILE, TILE), BF16),
        in_specs=[
            pl.BlockSpec(memory_space=pltpu.SMEM),
            pl.BlockSpec(memory_space=pltpu.VMEM),
        ],
        out_specs=pl.BlockSpec(memory_space=pltpu.VMEM),
        compiler_params=pltpu.CompilerParams(vmem_limit_bytes=16 << 20),
        name="pack_first",
    )(index, child)


def pack_second(index, tiles):
    def body(index_ref, tiles_ref, out_ref):
        for slot in range(64):
            out_ref[slot] = tiles_ref[index_ref[slot]]

    return pl.pallas_call(
        body,
        out_shape=jax.ShapeDtypeStruct((64, TILE, TILE), BF16),
        in_specs=[
            pl.BlockSpec(memory_space=pltpu.SMEM),
            pl.BlockSpec(memory_space=pltpu.VMEM),
        ],
        out_specs=pl.BlockSpec(memory_space=pltpu.VMEM),
        compiler_params=pltpu.CompilerParams(vmem_limit_bytes=16 << 20),
        name="pack_second",
    )(index, tiles)


def add_tiles(row_pos, col_pos, base, tiles):
    def body(row_ref, col_ref, base_ref, tiles_ref, out_ref):
        out_ref[...] = base_ref[...]
        for slot in range(64):
            rows = pl.ds(pl.multiple_of(row_ref[slot] * TILE, TILE), TILE)
            cols = pl.ds(pl.multiple_of(col_ref[slot] * TILE, TILE), TILE)
            out_ref[rows, cols] += tiles_ref[slot].astype(F32)

    return pl.pallas_call(
        body,
        out_shape=jax.ShapeDtypeStruct(base.shape, F32),
        in_specs=[
            pl.BlockSpec(memory_space=pltpu.SMEM),
            pl.BlockSpec(memory_space=pltpu.SMEM),
            pl.BlockSpec(memory_space=pltpu.VMEM),
            pl.BlockSpec(memory_space=pltpu.VMEM),
        ],
        out_specs=pl.BlockSpec(memory_space=pltpu.VMEM),
        compiler_params=pltpu.CompilerParams(vmem_limit_bytes=32 << 20),
        name="add_tiles",
    )(row_pos, col_pos, base, tiles)


def inverse_factor(diag_tiles):
    rows = []
    at = 0
    for s in range(4):
        parts = [diag_tiles[at + t] for t in range(s + 1)]
        at += s + 1
        parts += [jnp.zeros((TILE, TILE), F32)] * (3 - s)
        rows.append(jnp.concatenate(parts, axis=1))
    low = jnp.concatenate(rows, axis=0)
    full = jnp.tril(low) + jnp.tril(low, -1).T
    lower_f = jnp.linalg.cholesky(full, symmetrize_input=False)
    return jax.scipy.linalg.solve_triangular(lower_f, jnp.eye(KDIM, dtype=F32), lower=True)


def per_device(front_orig, child_update, tile_map):
    fr = lax.axis_index("front")
    r = lax.axis_index(ROW)
    c = lax.axis_index(COL)
    core = lax.axis_index("core")
    xlo = r % 2
    child_no = c // 4
    quarter = c % 4
    maps = tile_map.reshape(4, NCT)
    front = front_orig[0]

    my_cols = lax.dynamic_slice(maps, (child_no, 16 * quarter), (1, 16))[0]
    picked = []
    for s in range(4):
        hit = my_cols == s
        where_b = jnp.argmax(hit).astype(jnp.int32)
        strip = lax.dynamic_slice(child_update, (0, where_b * TILE), (4 * TILE, TILE))
        picked.append(jnp.where(jnp.any(hit), strip, jnp.zeros_like(strip)))
    picked = jnp.stack(picked).reshape(4, 4, 16, PIECE, TILE).transpose(2, 0, 1, 3, 4)
    picked = picked.reshape(16, 16 * PIECE, TILE)
    strip = front[:, :TILE].reshape(12, 16, PIECE, TILE).transpose(1, 0, 2, 3)
    strip = strip.reshape(16, 12 * PIECE, TILE)
    message = jnp.concatenate([picked, strip], axis=1)
    got = lax.all_to_all(message, COL, split_axis=0, concat_axis=0, tiled=True)
    child_piece = got[:, :128].reshape(4, 4, 128, TILE).astype(F32).sum(axis=1).astype(BF16)
    front_piece = got[:4, 128:].reshape(4, 12, PIECE, TILE)
    diag_piece = front_piece[:, 0].reshape(4 * PIECE, TILE)
    to_front = jnp.concatenate(
        [child_piece.reshape(2, 256, TILE), jnp.broadcast_to(diag_piece, (2, 32, TILE))], axis=1
    )
    message = jnp.broadcast_to(to_front[:, None], (2, 8, 288, TILE)).reshape(16, 288, TILE)
    got = lax.all_to_all(message, ("front",) + ROW, split_axis=0, concat_axis=0, tiled=True)
    blocks = got[:, :256].reshape(16, 2, 4, 4, PIECE, TILE)
    own_maps = lax.dynamic_slice(maps, (2 * fr, 0), (2, NCT))
    wanted = jnp.concatenate([r + 8 * jnp.arange(12), jnp.arange(4)])
    one_hot = (own_maps.reshape(1, 2, 16, 4) == wanted[:, None, None, None]).astype(BF16)
    added = jnp.einsum("tkna,nksapl->tspl", one_hot, blocks, preferred_element_type=F32)
    diag_front = lax.dynamic_slice(got, (8 * fr, 256, 0), (4, 32, TILE))
    front_part = jnp.concatenate(
        [front_piece.transpose(1, 0, 2, 3), diag_front.reshape(4, 4, PIECE, TILE)], axis=0
    )
    chunk = added + front_part.astype(F32)
    panel_chunk = chunk[:12].transpose(0, 2, 1, 3).reshape(12 * PIECE, KDIM)

    low_tiles = jnp.stack([chunk[12 + s, t] for s in range(4) for t in range(s + 1)])
    low_other = lax.ppermute(low_tiles, "core", [(0, 1), (1, 0)])
    first = jnp.where(core == 0, low_tiles, low_other)
    second = jnp.where(core == 0, low_other, low_tiles)
    low_pair = jnp.concatenate([first, second], axis=1)
    diag_all = lax.all_gather(low_pair, "z", axis=0)
    diag_tiles = diag_all.transpose(1, 0, 2, 3).reshape(10, TILE, TILE)
    panel_all = lax.all_gather(panel_chunk, COL, axis=0)

    inverse = inverse_factor(diag_tiles)

    a_no = jnp.arange(4)[:, None]
    x_to = (a_no // 2) ^ (quarter & 1)
    slots = (x_to * 16 + (my_cols % 16)[None, :]) * 2 + (a_no & 1)
    message = pack_first(slots.reshape(64).astype(jnp.int32), child_update)
    message = message.reshape(32, 2 * TILE, TILE)
    got = lax.all_to_all(message, ("xlo",) + COL, split_axis=0, concat_axis=0, tiled=True)
    class_of = jnp.argmax(
        (maps[:, None, :8] % 8) == jnp.arange(8)[None, :, None], axis=2
    ).astype(jnp.int32)
    kid = jnp.arange(4).reshape(2, 1, 2, 1)
    dest_row = jnp.arange(8).reshape(1, 8, 1, 1)
    half = jnp.arange(2).reshape(1, 1, 1, 2)
    klass = class_of[kid, dest_row]
    q_no = 2 * half + (((klass % 4) // 2) ^ xlo)
    source = ((klass // 4) * 16 + 4 * kid + q_no) * 2 + (klass & 1)
    message = pack_second(source.reshape(64).astype(jnp.int32), got.reshape(64, TILE, TILE))
    message = message.reshape(16, 4 * TILE, TILE)
    got = lax.all_to_all(message, ("front",) + ROW, split_axis=0, concat_axis=0, tiled=True)
    tiles = got.reshape(64, TILE, TILE)
    src_row = jnp.arange(16).reshape(16, 1, 1)
    sib = jnp.arange(2).reshape(1, 2, 1)
    half = jnp.arange(2).reshape(1, 1, 2)
    own_class = lax.dynamic_slice(class_of, (2 * fr, 0), (2, 8))[:, :]
    klass = jnp.take(own_class, r, axis=1).reshape(1, 2, 1)
    i_no = 4 * (2 * (src_row // 2) + klass // 4) + klass % 4
    q_no = 2 * half + (((klass % 4) // 2) ^ (src_row % 2))
    col_b = jnp.argmax((own_maps[:, :16] % 16) == c, axis=1).astype(jnp.int32).reshape(1, 2, 1)
    j_no = 16 * q_no + col_b
    full = (16, 2, 2)
    row_pos = own_maps[jnp.broadcast_to(sib, full), jnp.broadcast_to(i_no, full)] // 8
    col_pos = own_maps[jnp.broadcast_to(sib, full), jnp.broadcast_to(j_no, full)] // 16

    def dot_t(left, right, precision=HIGHEST):
        return lax.dot_general(
            left, right, (((1,), (1,)), ((), ())), precision=precision, preferred_element_type=F32
        )

    col_panel = jnp.arange(KDIM)[None, :] // PANEL
    g_chunk = dot_t(panel_chunk, inverse)
    chunk_t = jnp.repeat(r + 8 * jnp.arange(12), PIECE)[:, None]
    h_chunk = jnp.where(chunk_t >= 2 * (col_panel + 1), g_chunk, 0.0).astype(BF16)
    h_chunk = h_chunk.reshape(6, 2, PIECE, KDIM).transpose(1, 0, 2, 3)
    h_own = c // 8
    same = lax.dynamic_index_in_dim(h_chunk, h_own, 0, keepdims=False)
    cross = lax.dynamic_index_in_dim(h_chunk, 1 - h_own, 0, keepdims=False)
    route_same, route_cross = [], []
    for rr in range(8):
        for cc in range(16):
            h, m = cc // 8, cc % 8
            route_same.append((rr * 16 + cc, m * 16 + 8 * h + rr))
            route_cross.append((rr * 16 + cc, m * 16 + 8 * (1 - h) + rr))
    same = lax.ppermute(same, ROW + COL, route_same)
    cross = lax.ppermute(cross, ROW + COL, route_cross)
    piece = jnp.stack(
        [jnp.where(h_own == 0, same, cross), jnp.where(h_own == 0, cross, same)]
    )
    trail_cols = lax.all_gather(piece, ROW, axis=0)
    trail_cols = trail_cols.transpose(2, 1, 0, 3, 4).reshape(6 * TILE, KDIM)

    panel_rows = panel_all.reshape(16, 12, PIECE, KDIM).transpose(1, 0, 2, 3).reshape(12 * TILE, KDIM)
    row_t = jnp.repeat(r + 8 * jnp.arange(12), TILE)[:, None]
    factor = dot_t(panel_rows, inverse)
    factor = jnp.where(row_t >= 2 * col_panel, factor, 0.0)
    trail_rows = jnp.where(row_t >= 2 * (col_panel + 1), factor, 0.0)
    rows_hi = trail_rows.astype(BF16)
    rows_lo = (trail_rows - rows_hi.astype(F32)).astype(BF16)
    base = front.astype(F32) - dot_t(rows_hi, trail_cols, None) - dot_t(rows_lo, trail_cols, None)
    update = add_tiles(
        row_pos.reshape(64).astype(jnp.int32), col_pos.reshape(64).astype(jnp.int32), base, tiles
    )
    return (update[None], factor[None])


def solution(mesh):
    fine = Mesh(
        mesh.devices.reshape(2, 4, 2, 8, 2), ("front", "rowh", "xlo", "z", "core")
    )
    return jax.shard_map(
        per_device,
        mesh=fine,
        in_specs=(P("front", ROW, COL), P(("front",) + ROW, COL), P()),
        out_specs=(P("front", ROW, COL), P("front", ROW, None)),
        check_vma=False,
    )
```

```python
import functools

import jax
import jax.numpy as jnp
from jax import lax
from jax.experimental import pallas as pl
from jax.experimental.pallas import tpu as pltpu
from jax.sharding import Mesh
from jax.sharding import PartitionSpec as P

TILE = 128
PANEL = 256
KDIM = 512
NT = 96
NCT = 64
ROW = ("rowh", "xlo")
COL = ("z", "core")
PIECE = 8
F32 = jnp.float32
BF16 = jnp.bfloat16


def pack_first(place, maps, child, front):
    def body(place_ref, maps_ref, child_ref, front_ref, panel_ref, tiles_ref):
        child_no, quarter = place_ref[0], place_ref[1]
        targets = [maps_ref[child_no, 16 * quarter + b] for b in range(16)]

        def spread(block, at, count):
            for c in range(16):
                for n in range(0, count, 2):
                    pair = [block[m * TILE + 8 * c : m * TILE + 8 * c + 8] for m in (n, n + 1)]
                    panel_ref[c, at + 8 * n : at + 8 * n + 16, :] = jnp.concatenate(
                        pair, axis=0
                    ).astype(BF16)

        for s in range(4):
            found = jnp.int32(-1)
            for b in range(16):
                found = jnp.where(targets[b] == s, b, found)
            start = pl.multiple_of(jnp.maximum(found, 0) * TILE, TILE)
            strip = child_ref[:, pl.ds(start, TILE)].astype(F32)
            spread(jnp.where(found >= 0, strip, 0.0), 32 * s, 4)
        spread(front_ref[...].astype(F32), 128, 12)
        for b in range(16):
            col = targets[b] % 16
            for a in range(4):
                to = ((a // 2) ^ (quarter % 2)) * 32 + col * 2 + a % 2
                tile = child_ref[a * TILE : (a + 1) * TILE, b * TILE : (b + 1) * TILE]
                tiles_ref[to] = tile

    smem = pl.BlockSpec(memory_space=pltpu.SMEM)
    return pl.pallas_call(
        body,
        grid=(1,),
        out_shape=[
            jax.ShapeDtypeStruct((16, 224, TILE), BF16),
            jax.ShapeDtypeStruct((64, TILE, TILE), BF16),
        ],
        in_specs=[
            smem,
            smem,
            pl.BlockSpec(child.shape, lambda i: (0, 0)),
            pl.BlockSpec((12 * TILE, TILE), lambda i: (0, 0)),
        ],
        out_specs=[
            pl.BlockSpec((16, 224, TILE), lambda i: (0, 0, 0)),
            pl.BlockSpec((64, TILE, TILE), lambda i: (0, 0, 0)),
        ],
        compiler_params=pltpu.CompilerParams(vmem_limit_bytes=32 << 20),
        name="pack_first",
    )(place, maps, child, front)


def pack_second(index, tiles):
    def body(index_ref, tiles_ref, out_ref):
        for slot in range(64):
            out_ref[slot] = tiles_ref[index_ref[slot]]

    return pl.pallas_call(
        body,
        out_shape=jax.ShapeDtypeStruct((64, TILE, TILE), BF16),
        in_specs=[
            pl.BlockSpec(memory_space=pltpu.SMEM),
            pl.BlockSpec(memory_space=pltpu.VMEM),
        ],
        out_specs=pl.BlockSpec(memory_space=pltpu.VMEM),
        compiler_params=pltpu.CompilerParams(vmem_limit_bytes=16 << 20),
        name="pack_second",
    )(index, tiles)


def split_dot(left, right, dims):
    l_hi = left.astype(BF16)
    l_lo = (left - l_hi.astype(F32)).astype(BF16)
    r_hi = right.astype(BF16)
    r_lo = (right - r_hi.astype(F32)).astype(BF16)
    dot = functools.partial(
        lax.dot_general, dimension_numbers=(dims, ((), ())), preferred_element_type=F32
    )
    return dot(l_hi, r_hi) + (dot(l_hi, r_lo) + dot(l_lo, r_hi))


def inverse_factor(gathered):
    def body(piece_ref, w_ref, big, small):
        lane = lax.broadcasted_iota(jnp.int32, (TILE, 2 * KDIM), 1)
        sub8 = lax.broadcasted_iota(jnp.int32, (8, 2 * TILE), 0)
        for s in range(4):
            for piece in range(16):
                at = s * TILE + piece * 8
                for t in range(4):
                    row = (s * 4 + t) * 8
                    big[at : at + 8, t * TILE : (t + 1) * TILE] = piece_ref[piece, row : row + 8, :]
        row_no = lax.broadcasted_iota(jnp.int32, (KDIM, KDIM), 0)
        col_no = lax.broadcasted_iota(jnp.int32, (KDIM, KDIM), 1)
        big[:, KDIM:] = (row_no == col_no).astype(F32)
        eye = (
            lax.broadcasted_iota(jnp.int32, (TILE, TILE), 0)
            == lax.broadcasted_iota(jnp.int32, (TILE, TILE), 1)
        ).astype(F32)

        def block(j, carry):
            start = pl.multiple_of(j * TILE, TILE)
            rows = pl.ds(start, TILE)
            small[:, :TILE] = big[rows, pl.ds(start, TILE)]
            small[:, TILE:] = eye
            for b in range(TILE // 8):
                lo = 8 * b
                panel = small[lo : lo + 8, :]
                cols = [
                    jnp.broadcast_to(panel[:, lo + m : lo + m + 1], (8, TILE)) for m in range(8)
                ]
                for m in range(8):
                    pivot = jnp.broadcast_to(cols[m][m : m + 1], (8, TILE))
                    inv = lax.rsqrt(pivot)
                    inv = inv * (1.5 - 0.5 * pivot * inv * inv)
                    low = cols[m] * inv
                    for n in range(m + 1, 8):
                        cols[n] = cols[n] - low * (
                            jnp.broadcast_to(cols[n][m : m + 1], (8, TILE)) * inv
                        )
                    inv2 = jnp.concatenate([inv, inv], axis=1)
                    low2 = jnp.concatenate([low, low], axis=1)
                    scaled = jnp.broadcast_to(panel[m : m + 1], (8, 2 * TILE)) * inv2
                    panel = jnp.where(
                        sub8 > m, panel - low2 * scaled, jnp.where(sub8 == m, scaled, panel)
                    )
                small[lo : lo + 8, :] = panel
                if b < TILE // 8 - 1:
                    hi = panel.astype(BF16).astype(F32)
                    rest = panel - hi
                    left = jnp.concatenate([hi, hi, rest], axis=0)[:, :TILE].astype(BF16)
                    right = jnp.concatenate([hi, rest, hi], axis=0).astype(BF16)
                    change = lax.dot_general(
                        left, right, (((0,), (0,)), ((), ())), preferred_element_type=F32
                    )
                    small[lo + 8 :, :] = small[lo + 8 :, :] - change[lo + 8 :, :]
            upper = split_dot(small[:, TILE:], big[rows, :], ((1,), (0,)))
            big[rows, :] = upper
            below = jnp.where(lane >= start + TILE, upper, 0.0)[:, :KDIM]
            big[...] = big[...] - split_dot(below, upper, ((0,), (0,)))
            return carry

        lax.fori_loop(0, 4, block, 0)
        w_ref[...] = jnp.where(row_no >= col_no, big[:, KDIM:], 0.0)

    return pl.pallas_call(
        body,
        grid=(1,),
        out_shape=jax.ShapeDtypeStruct((KDIM, KDIM), F32),
        in_specs=[pl.BlockSpec((16, TILE, TILE), lambda i: (0, 0, 0))],
        out_specs=pl.BlockSpec((KDIM, KDIM), lambda i: (0, 0)),
        scratch_shapes=[
            pltpu.VMEM((KDIM, 2 * KDIM), F32),
            pltpu.VMEM((TILE, 2 * TILE), F32),
        ],
        compiler_params=pltpu.CompilerParams(vmem_limit_bytes=24 << 20),
        name="inverse_factor",
    )(gathered)


def solve_rows(first_tile, gathered, inverse):
    def body(tile_ref, piece_ref, w_ref, g_ref, hi_ref, lo_ref, rows, w_hi, w_lo):
        lt = pl.program_id(0)

        @pl.when(lt == 0)
        def _():
            hi = w_ref[...].astype(BF16)
            w_hi[...] = hi
            w_lo[...] = (w_ref[...] - hi.astype(F32)).astype(BF16)

        for piece in range(16):
            for s in range(4):
                rows[piece * 8 : piece * 8 + 8, s * TILE : (s + 1) * TILE] = piece_ref[
                    piece, s * 8 : s * 8 + 8, :
                ]
        f_hi = rows[...].astype(BF16)
        f_lo = (rows[...] - f_hi.astype(F32)).astype(BF16)
        dot = functools.partial(
            lax.dot_general,
            dimension_numbers=(((1,), (1,)), ((), ())),
            preferred_element_type=F32,
        )
        g = dot(f_hi, w_hi[...]) + (dot(f_hi, w_lo[...]) + dot(f_lo, w_hi[...]))
        tile_no = tile_ref[0] + 8 * lt
        panel_no = lax.broadcasted_iota(jnp.int32, (TILE, KDIM), 1) // PANEL
        g = jnp.where(tile_no >= 2 * panel_no, g, 0.0)
        g_ref[...] = g
        h = jnp.where(tile_no >= 2 * panel_no + 2, g, 0.0)
        h_hi = h.astype(BF16)
        hi_ref[...] = h_hi
        lo_ref[...] = (h - h_hi.astype(F32)).astype(BF16)

    rows_spec = pl.BlockSpec((TILE, KDIM), lambda lt, tile: (lt, 0))
    return pl.pallas_call(
        body,
        grid_spec=pltpu.PrefetchScalarGridSpec(
            num_scalar_prefetch=1,
            grid=(12,),
            in_specs=[
                pl.BlockSpec((16, 32, TILE), lambda lt, tile: (0, lt, 0)),
                pl.BlockSpec((KDIM, KDIM), lambda lt, tile: (0, 0)),
            ],
            out_specs=[rows_spec, rows_spec, rows_spec],
            scratch_shapes=[
                pltpu.VMEM((TILE, KDIM), F32),
                pltpu.VMEM((KDIM, KDIM), BF16),
                pltpu.VMEM((KDIM, KDIM), BF16),
            ],
        ),
        out_shape=[
            jax.ShapeDtypeStruct((12 * TILE, KDIM), F32),
            jax.ShapeDtypeStruct((12 * TILE, KDIM), BF16),
            jax.ShapeDtypeStruct((12 * TILE, KDIM), BF16),
        ],
        compiler_params=pltpu.CompilerParams(vmem_limit_bytes=24 << 20),
        name="solve_rows",
    )(first_tile, gathered, inverse)


def trailing_update(front, rows_hi, rows_lo, trail):
    def body(front_ref, hi_ref, lo_ref, trail_ref, out_ref, cols):
        @pl.when(pl.program_id(0) == 0)
        def _():
            for j in range(6):
                for p in range(0, 8, 2):
                    one = trail_ref[p, 16 * j : 16 * j + 16, :].astype(F32)
                    two = trail_ref[p + 1, 16 * j : 16 * j + 16, :].astype(F32)
                    for h in range(2):
                        at = j * TILE + 64 * h + 8 * p
                        both = jnp.concatenate(
                            [one[8 * h : 8 * h + 8], two[8 * h : 8 * h + 8]], axis=0
                        )
                        cols[at : at + 16, :] = both.astype(BF16)

        dot = functools.partial(
            lax.dot_general,
            dimension_numbers=(((1,), (1,)), ((), ())),
            preferred_element_type=F32,
        )
        out_ref[...] = front_ref[...].astype(F32) - (
            dot(hi_ref[...], cols[...]) + dot(lo_ref[...], cols[...])
        )

    width = front.shape[1]
    return pl.pallas_call(
        body,
        grid=(6,),
        in_specs=[
            pl.BlockSpec((2 * TILE, width), lambda n: (n, 0)),
            pl.BlockSpec((2 * TILE, KDIM), lambda n: (n, 0)),
            pl.BlockSpec((2 * TILE, KDIM), lambda n: (n, 0)),
            pl.BlockSpec((8, 96, KDIM), lambda n: (0, 0, 0)),
        ],
        out_specs=pl.BlockSpec((2 * TILE, width), lambda n: (n, 0)),
        scratch_shapes=[pltpu.VMEM((6 * TILE, KDIM), BF16)],
        out_shape=jax.ShapeDtypeStruct(front.shape, F32),
        compiler_params=pltpu.CompilerParams(vmem_limit_bytes=24 << 20),
        name="trailing_update",
    )(front, rows_hi, rows_lo, trail)


def add_tiles(tile_at, col_at, base, tiles):
    def body(at_ref, col_ref, base_ref, tiles_ref, out_ref):
        lt = pl.program_id(0)
        out_ref[...] = base_ref[...]
        for n in range(8):
            source = at_ref[lt * 8 + n]

            @pl.when(source >= 0)
            def _():
                where_col = pl.multiple_of(col_ref[lt * 8 + n] * TILE, TILE)
                out_ref[:, pl.ds(where_col, TILE)] += tiles_ref[source].astype(F32)

    width = base.shape[1]
    return pl.pallas_call(
        body,
        grid_spec=pltpu.PrefetchScalarGridSpec(
            num_scalar_prefetch=2,
            grid=(12,),
            in_specs=[
                pl.BlockSpec((TILE, width), lambda lt, a, b: (lt, 0)),
                pl.BlockSpec((64, TILE, TILE), lambda lt, a, b: (0, 0, 0)),
            ],
            out_specs=pl.BlockSpec((TILE, width), lambda lt, a, b: (lt, 0)),
        ),
        out_shape=jax.ShapeDtypeStruct(base.shape, F32),
        compiler_params=pltpu.CompilerParams(vmem_limit_bytes=24 << 20),
        name="add_tiles",
    )(tile_at, col_at, base, tiles)


def per_device(front_orig, child_update, tile_map):
    fr = lax.axis_index("front")
    r = lax.axis_index(ROW)
    c = lax.axis_index(COL)
    xlo = r % 2
    child_no = c // 4
    quarter = c % 4
    maps = tile_map.reshape(4, NCT)
    front = front_orig[0]

    place = jnp.stack([child_no, quarter]).astype(jnp.int32)
    message, first_tiles = pack_first(place, maps, child_update, front)
    got = lax.all_to_all(message, COL, split_axis=0, concat_axis=0, tiled=True)
    child_piece = got[:, :128].reshape(4, 4, 128, TILE).astype(F32).sum(axis=1).astype(BF16)
    front_piece = got[:4, 128:].reshape(4, 12, PIECE, TILE)
    diag_piece = front_piece[:, 0].reshape(4 * PIECE, TILE)
    to_front = jnp.concatenate(
        [child_piece.reshape(2, 256, TILE), jnp.broadcast_to(diag_piece, (2, 32, TILE))], axis=1
    )
    message = jnp.broadcast_to(to_front[:, None], (2, 8, 288, TILE)).reshape(16, 288, TILE)
    got = lax.all_to_all(message, ("front",) + ROW, split_axis=0, concat_axis=0, tiled=True)
    blocks = got[:, :256].reshape(16, 2, 4, 4, PIECE, TILE)
    own_maps = lax.dynamic_slice(maps, (2 * fr, 0), (2, NCT))
    wanted = jnp.concatenate([r + 8 * jnp.arange(12), jnp.arange(4)])
    one_hot = (own_maps.reshape(1, 2, 16, 4) == wanted[:, None, None, None]).astype(BF16)
    added = jnp.einsum("tkna,nksapl->tspl", one_hot, blocks, preferred_element_type=F32)
    diag_front = lax.dynamic_slice(got, (8 * fr, 256, 0), (4, 32, TILE))
    front_part = jnp.concatenate(
        [front_piece.transpose(1, 0, 2, 3), diag_front.reshape(4, 4, PIECE, TILE)], axis=0
    )
    chunk = added + front_part.astype(F32)
    diag_all = lax.all_gather(chunk[12:].reshape(128, TILE), COL, axis=0)
    panel_all = lax.all_gather(chunk[:12].reshape(384, TILE), COL, axis=0)
    inverse = inverse_factor(diag_all)

    panel_chunk = chunk[:12].transpose(0, 2, 1, 3).reshape(12 * PIECE, KDIM)
    g_chunk = lax.dot_general(
        panel_chunk,
        inverse,
        (((1,), (1,)), ((), ())),
        precision=lax.Precision.HIGHEST,
        preferred_element_type=F32,
    )
    chunk_t = jnp.repeat(r + 8 * jnp.arange(12), PIECE)[:, None]
    after = 2 * (jnp.arange(KDIM)[None, :] // PANEL) + 2
    h_chunk = jnp.where(chunk_t >= after, g_chunk, 0.0).astype(BF16)
    h_chunk = h_chunk.reshape(6, 2, PIECE, KDIM).transpose(1, 0, 2, 3)
    h_own = c // 8
    same = lax.dynamic_index_in_dim(h_chunk, h_own, 0, keepdims=False)
    cross = lax.dynamic_index_in_dim(h_chunk, 1 - h_own, 0, keepdims=False)
    route_same, route_cross = [], []
    for rr in range(8):
        for cc in range(16):
            h, m = cc // 8, cc % 8
            route_same.append((rr * 16 + cc, m * 16 + 8 * h + rr))
            route_cross.append((rr * 16 + cc, m * 16 + 8 * (1 - h) + rr))
    same = lax.ppermute(same, ROW + COL, route_same)
    cross = lax.ppermute(cross, ROW + COL, route_cross)
    first = jnp.where(h_own == 0, same, cross)
    second = jnp.where(h_own == 0, cross, same)
    piece = jnp.concatenate([first, second], axis=1).reshape(96, KDIM)
    trail = lax.all_to_all(
        jnp.broadcast_to(piece, (8, 96, KDIM)), ROW, split_axis=0, concat_axis=0, tiled=True
    )

    message = first_tiles.reshape(32, 2 * TILE, TILE)
    got = lax.all_to_all(message, ("xlo",) + COL, split_axis=0, concat_axis=0, tiled=True)
    got, trail = lax.optimization_barrier((got, trail))
    class_of = jnp.argmax(
        (maps[:, None, :8] % 8) == jnp.arange(8)[None, :, None], axis=2
    ).astype(jnp.int32)
    kid = jnp.arange(4).reshape(2, 1, 2, 1)
    dest_row = jnp.arange(8).reshape(1, 8, 1, 1)
    half = jnp.arange(2).reshape(1, 1, 1, 2)
    klass = class_of[kid, dest_row]
    q_no = 2 * half + (((klass % 4) // 2) ^ xlo)
    source = ((klass // 4) * 16 + 4 * kid + q_no) * 2 + (klass & 1)
    message = pack_second(source.reshape(64).astype(jnp.int32), got.reshape(64, TILE, TILE))
    message = message.reshape(16, 4 * TILE, TILE)
    got = lax.all_to_all(message, ("front",) + ROW, split_axis=0, concat_axis=0, tiled=True)
    tiles = got.reshape(64, TILE, TILE)
    match = own_maps[None] == (r + 8 * jnp.arange(12))[:, None, None]
    i_no = jnp.argmax(match, axis=2).astype(jnp.int32)[:, :, None, None]
    present = jnp.any(match, axis=2)[:, :, None, None]
    sib = jnp.arange(2).reshape(1, 2, 1, 1)
    x_from = jnp.arange(2).reshape(1, 1, 2, 1)
    half = jnp.arange(2).reshape(1, 1, 1, 2)
    sender = (i_no // 32) * 8 + (i_no % 32) // 8 * 2 + x_from
    tile_at = jnp.where(present, (sender * 2 + sib) * 2 + half, -1)
    col_b = jnp.argmax((own_maps[:, :16] % 16) == c, axis=1).astype(jnp.int32)
    col_tiles = own_maps.reshape(2, 4, 16)
    col_tiles = jnp.take_along_axis(col_tiles, col_b.reshape(2, 1, 1), axis=2)[:, :, 0] // 16
    q_no = 2 * half + (((i_no % 4) // 2) ^ x_from)
    col_at = jnp.zeros(q_no.shape[:1] + (2, 2, 2), jnp.int32)
    for q in range(4):
        col_at = jnp.where(q_no == q, col_tiles[:, q].reshape(1, 2, 1, 1), col_at)

    factor, rows_hi, rows_lo = solve_rows(r.reshape(1).astype(jnp.int32), panel_all, inverse)
    base = trailing_update(front, rows_hi, rows_lo, trail)
    update = add_tiles(
        tile_at.reshape(96).astype(jnp.int32), col_at.reshape(96).astype(jnp.int32), base, tiles
    )
    return (update[None], factor[None])


def solution(mesh):
    fine = Mesh(
        mesh.devices.reshape(2, 4, 2, 8, 2), ("front", "rowh", "xlo", "z", "core")
    )
    return jax.shard_map(
        per_device,
        mesh=fine,
        in_specs=(P("front", ROW, COL), P(("front",) + ROW, COL), P()),
        out_specs=(P("front", ROW, COL), P("front", ROW, None)),
        check_vma=False,
    )
```

```python
import functools

import jax
import jax.numpy as jnp
from jax import lax
from jax.experimental import pallas as pl
from jax.experimental.pallas import tpu as pltpu
from jax.sharding import Mesh
from jax.sharding import PartitionSpec as P

TILE = 128
PANEL = 256
KDIM = 512
NT = 96
NCT = 64
ROW = ("rowh", "xlo")
COL = ("z", "core")
PIECE = 8
F32 = jnp.float32
BF16 = jnp.bfloat16


def pack_panel(place, maps, child, front):
    def locate(s, place_ref, maps_ref):
        found = jnp.int32(-1)
        for b in range(16):
            target = maps_ref[place_ref[0], 16 * place_ref[1] + b]
            found = jnp.where(target == s, b, found)
        return found

    def body(place_ref, maps_ref, *refs):
        strips, front_ref, panel_ref = refs[:4], refs[4], refs[5]

        def spread(block, at, count):
            for c in range(16):
                for n in range(0, count, 2):
                    pair = [block[m * TILE + 8 * c : m * TILE + 8 * c + 8] for m in (n, n + 1)]
                    panel_ref[c, at + 8 * n : at + 8 * n + 16, :] = jnp.concatenate(
                        pair, axis=0
                    ).astype(BF16)

        for s in range(4):
            strip = strips[s][...].astype(F32)
            spread(jnp.where(locate(s, place_ref, maps_ref) >= 0, strip, 0.0), 32 * s, 4)
        spread(front_ref[...].astype(F32), 128, 12)

    def strip_spec(s):
        return pl.BlockSpec(
            (4 * TILE, TILE), lambda i, p, m: (0, jnp.maximum(locate(s, p, m), 0))
        )

    return pl.pallas_call(
        body,
        grid_spec=pltpu.PrefetchScalarGridSpec(
            num_scalar_prefetch=2,
            grid=(1,),
            in_specs=[strip_spec(s) for s in range(4)]
            + [pl.BlockSpec((12 * TILE, TILE), lambda i, p, m: (0, 0))],
            out_specs=pl.BlockSpec((16, 224, TILE), lambda i, p, m: (0, 0, 0)),
        ),
        out_shape=jax.ShapeDtypeStruct((16, 224, TILE), BF16),
        compiler_params=pltpu.CompilerParams(vmem_limit_bytes=56 << 20),
        name="pack_panel",
    )(place, maps, child, child, child, child, front)


def pack_first(place, maps, child):
    def body(place_ref, maps_ref, child_ref, tiles_ref):
        child_no, quarter = place_ref[0], place_ref[1]
        for b in range(16):
            col = maps_ref[child_no, 16 * quarter + b] % 16
            for a in range(4):
                to = ((a // 2) ^ (quarter % 2)) * 32 + col * 2 + a % 2
                tile = child_ref[a * TILE : (a + 1) * TILE, b * TILE : (b + 1) * TILE]
                tiles_ref[to] = tile

    smem = pl.BlockSpec(memory_space=pltpu.SMEM)
    return pl.pallas_call(
        body,
        grid=(1,),
        out_shape=jax.ShapeDtypeStruct((64, TILE, TILE), BF16),
        in_specs=[smem, smem, pl.BlockSpec(child.shape, lambda i: (0, 0))],
        out_specs=pl.BlockSpec((64, TILE, TILE), lambda i: (0, 0, 0)),
        compiler_params=pltpu.CompilerParams(vmem_limit_bytes=14 << 20),
        cost_estimate=pl.CostEstimate(flops=0, bytes_accessed=4 << 20, transcendentals=0),
        name="pack_first",
    )(place, maps, child)


def pack_second(index, tiles):
    def body(index_ref, tiles_ref, out_ref):
        for slot in range(64):
            out_ref[slot] = tiles_ref[index_ref[slot]]

    return pl.pallas_call(
        body,
        out_shape=jax.ShapeDtypeStruct((64, TILE, TILE), BF16),
        in_specs=[
            pl.BlockSpec(memory_space=pltpu.SMEM),
            pl.BlockSpec(memory_space=pltpu.VMEM),
        ],
        out_specs=pl.BlockSpec(memory_space=pltpu.VMEM),
        compiler_params=pltpu.CompilerParams(vmem_limit_bytes=10 << 20),
        name="pack_second",
    )(index, tiles)


def split_dot(left, right, dims):
    l_hi = left.astype(BF16)
    l_lo = (left - l_hi.astype(F32)).astype(BF16)
    r_hi = right.astype(BF16)
    r_lo = (right - r_hi.astype(F32)).astype(BF16)
    dot = functools.partial(
        lax.dot_general, dimension_numbers=(dims, ((), ())), preferred_element_type=F32
    )
    return dot(l_hi, r_hi) + (dot(l_hi, r_lo) + dot(l_lo, r_hi))


def inverse_factor(gathered):
    group = 16

    def body(piece_ref, w_ref, big, small):
        lane = lax.broadcasted_iota(jnp.int32, (group, TILE), 1)
        sub = lax.broadcasted_iota(jnp.int32, (group, TILE), 0)
        lane_all = lax.broadcasted_iota(jnp.int32, (TILE, TILE), 1)
        row_all = lax.broadcasted_iota(jnp.int32, (TILE, TILE), 0)
        for s in range(4):
            for piece in range(16):
                at = s * TILE + piece * 8
                for t in range(4):
                    row = (s * 4 + t) * 8
                    big[at : at + 8, t * TILE : (t + 1) * TILE] = piece_ref[piece, row : row + 8, :]

        for j in range(4):
            start = j * TILE
            stop = start + TILE
            small[...] = big[start:stop, start:stop]
            for b in range(TILE // group):
                lo = group * b
                panel = small[lo : lo + group, :]
                unit = jnp.where(lane == sub + lo, 1.0, 0.0)
                cols = [
                    jnp.broadcast_to(panel[:, lo + m : lo + m + 1], (group, TILE))
                    for m in range(group)
                ]
                for m in range(group):
                    inv = lax.rsqrt(jnp.broadcast_to(cols[m][m : m + 1], (group, TILE)))
                    low = cols[m] * inv
                    for n in range(m + 1, group):
                        cols[n] = cols[n] - low * (
                            jnp.broadcast_to(cols[n][m : m + 1], (group, TILE)) * inv
                        )
                    low = jnp.where(sub > m, low, 0.0)
                    keep = jnp.where(sub == m, inv, 1.0)
                    panel = panel * keep - low * (
                        jnp.broadcast_to(panel[m : m + 1], (group, TILE)) * inv
                    )
                    unit = unit * keep - low * (
                        jnp.broadcast_to(unit[m : m + 1], (group, TILE)) * inv
                    )
                here = (lane >= lo) & (lane < lo + group)
                final = jnp.where(here, unit, panel)
                small[lo : lo + group, :] = final
                if lo + group < TILE:
                    p_hi = panel.astype(BF16).astype(F32)
                    f_hi = final.astype(BF16).astype(F32)
                    left = jnp.concatenate([p_hi, p_hi, panel - p_hi], axis=0).astype(BF16)
                    right = jnp.concatenate([f_hi, final - f_hi, f_hi], axis=0).astype(BF16)
                    change = lax.dot_general(
                        left, right, (((0,), (0,)), ((), ())), preferred_element_type=F32
                    )
                    rest = small[lo + group :, :]
                    in_block = lane_all[lo + group :, :]
                    in_block = (in_block >= lo) & (in_block < lo + group)
                    small[lo + group :, :] = jnp.where(in_block, 0.0, rest) - change[lo + group :, :]
            diag = jnp.where(row_all >= lane_all, small[...], 0.0)
            if j > 0:
                left_part = split_dot(diag, big[start:stop, :start], ((1,), (0,)))
                big[start:stop, :start] = left_part
            if j < 3:
                upper = split_dot(diag, big[start:stop, stop:], ((1,), (0,)))
                if j > 0:
                    big[stop:, :start] -= split_dot(upper, left_part, ((0,), (0,)))
                big[stop:, start:stop] = -split_dot(upper, diag, ((0,), (0,)))
                big[stop:, stop:] -= split_dot(upper, upper, ((0,), (0,)))
                big[start:stop, stop:] = jnp.zeros((TILE, KDIM - stop), F32)
            big[start:stop, start:stop] = diag
        w_ref[...] = big[...]

    return pl.pallas_call(
        body,
        grid=(1,),
        out_shape=jax.ShapeDtypeStruct((KDIM, KDIM), F32),
        in_specs=[pl.BlockSpec((16, TILE, TILE), lambda i: (0, 0, 0))],
        out_specs=pl.BlockSpec((KDIM, KDIM), lambda i: (0, 0)),
        scratch_shapes=[
            pltpu.VMEM((KDIM, KDIM), F32),
            pltpu.VMEM((TILE, TILE), F32),
        ],
        compiler_params=pltpu.CompilerParams(vmem_limit_bytes=16 << 20),
        name="inverse_factor",
    )(gathered)


def solve_rows(first_tile, gathered, inverse):
    def body(tile_ref, piece_ref, w_ref, g_ref, hi_ref, lo_ref, rows, w_hi, w_lo):
        lt = pl.program_id(0)

        @pl.when(lt == 0)
        def _():
            hi = w_ref[...].astype(BF16)
            w_hi[...] = hi
            w_lo[...] = (w_ref[...] - hi.astype(F32)).astype(BF16)

        for piece in range(16):
            for s in range(4):
                rows[piece * 8 : piece * 8 + 8, s * TILE : (s + 1) * TILE] = piece_ref[
                    piece, s * 8 : s * 8 + 8, :
                ]
        f_hi = rows[...].astype(BF16)
        f_lo = (rows[...] - f_hi.astype(F32)).astype(BF16)
        dot = functools.partial(
            lax.dot_general,
            dimension_numbers=(((1,), (1,)), ((), ())),
            preferred_element_type=F32,
        )
        g = dot(f_hi, w_hi[...]) + (dot(f_hi, w_lo[...]) + dot(f_lo, w_hi[...]))
        tile_no = tile_ref[0] + 8 * lt
        panel_no = lax.broadcasted_iota(jnp.int32, (TILE, KDIM), 1) // PANEL
        g = jnp.where(tile_no >= 2 * panel_no, g, 0.0)
        g_ref[...] = g
        h = jnp.where(tile_no >= 2 * panel_no + 2, g, 0.0)
        h_hi = h.astype(BF16)
        hi_ref[...] = h_hi
        lo_ref[...] = (h - h_hi.astype(F32)).astype(BF16)

    rows_spec = pl.BlockSpec((TILE, KDIM), lambda lt, tile: (lt, 0))
    return pl.pallas_call(
        body,
        grid_spec=pltpu.PrefetchScalarGridSpec(
            num_scalar_prefetch=1,
            grid=(12,),
            in_specs=[
                pl.BlockSpec((16, 32, TILE), lambda lt, tile: (0, lt, 0)),
                pl.BlockSpec((KDIM, KDIM), lambda lt, tile: (0, 0)),
            ],
            out_specs=[rows_spec, rows_spec, rows_spec],
            scratch_shapes=[
                pltpu.VMEM((TILE, KDIM), F32),
                pltpu.VMEM((KDIM, KDIM), BF16),
                pltpu.VMEM((KDIM, KDIM), BF16),
            ],
        ),
        out_shape=[
            jax.ShapeDtypeStruct((12 * TILE, KDIM), F32),
            jax.ShapeDtypeStruct((12 * TILE, KDIM), BF16),
            jax.ShapeDtypeStruct((12 * TILE, KDIM), BF16),
        ],
        compiler_params=pltpu.CompilerParams(vmem_limit_bytes=10 << 20),
        name="solve_rows",
    )(first_tile, gathered, inverse)


def trailing_update(front, rows_hi, rows_lo, trail):
    def body(front_ref, hi_ref, lo_ref, trail_ref, out_ref, cols):
        @pl.when(pl.program_id(0) == 0)
        def _():
            for j in range(6):
                for p in range(0, 8, 2):
                    one = trail_ref[p, 16 * j : 16 * j + 16, :].astype(F32)
                    two = trail_ref[p + 1, 16 * j : 16 * j + 16, :].astype(F32)
                    for h in range(2):
                        at = j * TILE + 64 * h + 8 * p
                        both = jnp.concatenate(
                            [one[8 * h : 8 * h + 8], two[8 * h : 8 * h + 8]], axis=0
                        )
                        cols[at : at + 16, :] = both.astype(BF16)

        dot = functools.partial(
            lax.dot_general,
            dimension_numbers=(((1,), (1,)), ((), ())),
            preferred_element_type=F32,
        )
        out_ref[...] = front_ref[...].astype(F32) - (
            dot(hi_ref[...], cols[...]) + dot(lo_ref[...], cols[...])
        )

    width = front.shape[1]
    return pl.pallas_call(
        body,
        grid=(6,),
        in_specs=[
            pl.BlockSpec((2 * TILE, width), lambda n: (n, 0)),
            pl.BlockSpec((2 * TILE, KDIM), lambda n: (n, 0)),
            pl.BlockSpec((2 * TILE, KDIM), lambda n: (n, 0)),
            pl.BlockSpec((8, 96, KDIM), lambda n: (0, 0, 0)),
        ],
        out_specs=pl.BlockSpec((2 * TILE, width), lambda n: (n, 0)),
        scratch_shapes=[pltpu.VMEM((6 * TILE, KDIM), BF16)],
        out_shape=jax.ShapeDtypeStruct(front.shape, F32),
        compiler_params=pltpu.CompilerParams(vmem_limit_bytes=10 << 20),
        name="trailing_update",
    )(front, rows_hi, rows_lo, trail)


def add_tiles(tile_at, col_at, base, tiles):
    def body(at_ref, col_ref, base_ref, tiles_ref, out_ref):
        lt = pl.program_id(0)
        out_ref[...] = base_ref[...]
        for n in range(8):
            source = at_ref[lt * 8 + n]

            @pl.when(source >= 0)
            def _():
                where_col = pl.multiple_of(col_ref[lt * 8 + n] * TILE, TILE)
                out_ref[:, pl.ds(where_col, TILE)] += tiles_ref[source].astype(F32)

    width = base.shape[1]
    return pl.pallas_call(
        body,
        grid_spec=pltpu.PrefetchScalarGridSpec(
            num_scalar_prefetch=2,
            grid=(12,),
            in_specs=[
                pl.BlockSpec((TILE, width), lambda lt, a, b: (lt, 0)),
                pl.BlockSpec((64, TILE, TILE), lambda lt, a, b: (0, 0, 0)),
            ],
            out_specs=pl.BlockSpec((TILE, width), lambda lt, a, b: (lt, 0)),
        ),
        out_shape=jax.ShapeDtypeStruct(base.shape, F32),
        compiler_params=pltpu.CompilerParams(vmem_limit_bytes=10 << 20),
        name="add_tiles",
    )(tile_at, col_at, base, tiles)


def per_device(front_orig, child_update, tile_map):
    fr = lax.axis_index("front")
    r = lax.axis_index(ROW)
    c = lax.axis_index(COL)
    xlo = r % 2
    child_no = c // 4
    quarter = c % 4
    maps = tile_map.reshape(4, NCT)
    front = front_orig[0]

    place = jnp.stack([child_no, quarter]).astype(jnp.int32)
    message = pack_panel(place, maps, child_update, front)
    first_tiles = pack_first(place, maps, child_update)
    got = lax.all_to_all(message, COL, split_axis=0, concat_axis=0, tiled=True)
    child_piece = got[:, :128].reshape(4, 4, 128, TILE).astype(F32).sum(axis=1).astype(BF16)
    front_piece = got[:4, 128:].reshape(4, 12, PIECE, TILE)
    diag_piece = front_piece[:, 0].reshape(4 * PIECE, TILE)
    to_front = jnp.concatenate(
        [child_piece.reshape(2, 256, TILE), jnp.broadcast_to(diag_piece, (2, 32, TILE))], axis=1
    )
    message = jnp.broadcast_to(to_front[:, None], (2, 8, 288, TILE)).reshape(16, 288, TILE)
    got = lax.all_to_all(message, ("front",) + ROW, split_axis=0, concat_axis=0, tiled=True)
    blocks = got[:, :256].reshape(16, 2, 4, 4, PIECE, TILE)
    own_maps = lax.dynamic_slice(maps, (2 * fr, 0), (2, NCT))
    wanted = jnp.concatenate([r + 8 * jnp.arange(12), jnp.arange(4)])
    one_hot = (own_maps.reshape(1, 2, 16, 4) == wanted[:, None, None, None]).astype(BF16)
    added = jnp.einsum("tkna,nksapl->tspl", one_hot, blocks, preferred_element_type=F32)
    diag_front = lax.dynamic_slice(got, (8 * fr, 256, 0), (4, 32, TILE))
    front_part = jnp.concatenate(
        [front_piece.transpose(1, 0, 2, 3), diag_front.reshape(4, 4, PIECE, TILE)], axis=0
    )
    chunk = added + front_part.astype(F32)
    diag_all = lax.all_gather(chunk[12:].reshape(128, TILE), COL, axis=0)
    panel_all = lax.all_gather(chunk[:12].reshape(384, TILE), COL, axis=0)
    inverse = inverse_factor(diag_all)

    panel_chunk = chunk[:12].transpose(0, 2, 1, 3).reshape(12 * PIECE, KDIM)
    g_chunk = lax.dot_general(
        panel_chunk,
        inverse,
        (((1,), (1,)), ((), ())),
        precision=lax.Precision.HIGHEST,
        preferred_element_type=F32,
    )
    chunk_t = jnp.repeat(r + 8 * jnp.arange(12), PIECE)[:, None]
    after = 2 * (jnp.arange(KDIM)[None, :] // PANEL) + 2
    h_chunk = jnp.where(chunk_t >= after, g_chunk, 0.0).astype(BF16)
    h_chunk = h_chunk.reshape(6, 2, PIECE, KDIM).transpose(1, 0, 2, 3)
    h_own = c // 8
    same = lax.dynamic_index_in_dim(h_chunk, h_own, 0, keepdims=False)
    cross = lax.dynamic_index_in_dim(h_chunk, 1 - h_own, 0, keepdims=False)
    route_same, route_cross = [], []
    for rr in range(8):
        for cc in range(16):
            h, m = cc // 8, cc % 8
            route_same.append((rr * 16 + cc, m * 16 + 8 * h + rr))
            route_cross.append((rr * 16 + cc, m * 16 + 8 * (1 - h) + rr))
    same = lax.ppermute(same, ROW + COL, route_same)
    cross = lax.ppermute(cross, ROW + COL, route_cross)
    first = jnp.where(h_own == 0, same, cross)
    second = jnp.where(h_own == 0, cross, same)
    piece = jnp.concatenate([first, second], axis=1).reshape(96, KDIM)
    trail = lax.all_to_all(
        jnp.broadcast_to(piece, (8, 96, KDIM)), ROW, split_axis=0, concat_axis=0, tiled=True
    )

    message = first_tiles.reshape(32, 2 * TILE, TILE)
    got = lax.all_to_all(message, ("xlo",) + COL, split_axis=0, concat_axis=0, tiled=True)
    got, trail = lax.optimization_barrier((got, trail))
    class_of = jnp.argmax(
        (maps[:, None, :8] % 8) == jnp.arange(8)[None, :, None], axis=2
    ).astype(jnp.int32)
    kid = jnp.arange(4).reshape(2, 1, 2, 1)
    dest_row = jnp.arange(8).reshape(1, 8, 1, 1)
    half = jnp.arange(2).reshape(1, 1, 1, 2)
    klass = class_of[kid, dest_row]
    q_no = 2 * half + (((klass % 4) // 2) ^ xlo)
    source = ((klass // 4) * 16 + 4 * kid + q_no) * 2 + (klass & 1)
    message = pack_second(source.reshape(64).astype(jnp.int32), got.reshape(64, TILE, TILE))
    message = message.reshape(16, 4 * TILE, TILE)
    got = lax.all_to_all(message, ("front",) + ROW, split_axis=0, concat_axis=0, tiled=True)
    tiles = got.reshape(64, TILE, TILE)
    match = own_maps[None] == (r + 8 * jnp.arange(12))[:, None, None]
    i_no = jnp.argmax(match, axis=2).astype(jnp.int32)[:, :, None, None]
    present = jnp.any(match, axis=2)[:, :, None, None]
    sib = jnp.arange(2).reshape(1, 2, 1, 1)
    x_from = jnp.arange(2).reshape(1, 1, 2, 1)
    half = jnp.arange(2).reshape(1, 1, 1, 2)
    sender = (i_no // 32) * 8 + (i_no % 32) // 8 * 2 + x_from
    tile_at = jnp.where(present, (sender * 2 + sib) * 2 + half, -1)
    col_b = jnp.argmax((own_maps[:, :16] % 16) == c, axis=1).astype(jnp.int32)
    col_tiles = own_maps.reshape(2, 4, 16)
    col_tiles = jnp.take_along_axis(col_tiles, col_b.reshape(2, 1, 1), axis=2)[:, :, 0] // 16
    q_no = 2 * half + (((i_no % 4) // 2) ^ x_from)
    col_at = jnp.zeros(q_no.shape[:1] + (2, 2, 2), jnp.int32)
    for q in range(4):
        col_at = jnp.where(q_no == q, col_tiles[:, q].reshape(1, 2, 1, 1), col_at)

    factor, rows_hi, rows_lo = solve_rows(r.reshape(1).astype(jnp.int32), panel_all, inverse)
    base = trailing_update(front, rows_hi, rows_lo, trail)
    update = add_tiles(
        tile_at.reshape(96).astype(jnp.int32), col_at.reshape(96).astype(jnp.int32), base, tiles
    )
    return (update[None], factor[None])


def solution(mesh):
    fine = Mesh(
        mesh.devices.reshape(2, 4, 2, 8, 2), ("front", "rowh", "xlo", "z", "core")
    )
    return jax.shard_map(
        per_device,
        mesh=fine,
        in_specs=(P("front", ROW, COL), P(("front",) + ROW, COL), P()),
        out_specs=(P("front", ROW, COL), P("front", ROW, None)),
        check_vma=False,
    )
```

```python
import functools

import jax
import jax.numpy as jnp
from jax import lax
from jax.experimental import pallas as pl
from jax.experimental.pallas import tpu as pltpu
from jax.sharding import Mesh
from jax.sharding import PartitionSpec as P

TILE = 128
PANEL = 256
KDIM = 512
NT = 96
NCT = 64
ROW = ("rowh", "xlo")
COL = ("z", "core")
PIECE = 8
F32 = jnp.float32
BF16 = jnp.bfloat16


def pack_panel(place, maps, child, front):
    def locate(s, place_ref, maps_ref):
        found = jnp.int32(-1)
        for b in range(16):
            target = maps_ref[place_ref[0], 16 * place_ref[1] + b]
            found = jnp.where(target == s, b, found)
        return found

    def body(place_ref, maps_ref, *refs):
        strips, front_ref, panel_ref = refs[:4], refs[4], refs[5]

        def spread(block, at, count):
            for c in range(16):
                for n in range(0, count, 2):
                    pair = [block[m * TILE + 8 * c : m * TILE + 8 * c + 8] for m in (n, n + 1)]
                    panel_ref[c, at + 8 * n : at + 8 * n + 16, :] = jnp.concatenate(
                        pair, axis=0
                    ).astype(BF16)

        for s in range(4):
            strip = strips[s][...].astype(F32)
            spread(jnp.where(locate(s, place_ref, maps_ref) >= 0, strip, 0.0), 32 * s, 4)
        spread(front_ref[...].astype(F32), 128, 12)

    def strip_spec(s):
        return pl.BlockSpec(
            (4 * TILE, TILE), lambda i, p, m: (0, jnp.maximum(locate(s, p, m), 0))
        )

    return pl.pallas_call(
        body,
        grid_spec=pltpu.PrefetchScalarGridSpec(
            num_scalar_prefetch=2,
            grid=(1,),
            in_specs=[strip_spec(s) for s in range(4)]
            + [pl.BlockSpec((12 * TILE, TILE), lambda i, p, m: (0, 0))],
            out_specs=pl.BlockSpec((16, 224, TILE), lambda i, p, m: (0, 0, 0)),
        ),
        out_shape=jax.ShapeDtypeStruct((16, 224, TILE), BF16),
        compiler_params=pltpu.CompilerParams(vmem_limit_bytes=56 << 20),
        name="pack_panel",
    )(place, maps, child, child, child, child, front)


def pack_first(place, maps, child):
    def body(place_ref, maps_ref, child_ref, tiles_ref):
        child_no, quarter = place_ref[0], place_ref[1]
        for b in range(16):
            col = maps_ref[child_no, 16 * quarter + b] % 16
            for a in range(4):
                to = ((a // 2) ^ (quarter % 2)) * 32 + col * 2 + a % 2
                tile = child_ref[a * TILE : (a + 1) * TILE, b * TILE : (b + 1) * TILE]
                tiles_ref[to] = tile

    smem = pl.BlockSpec(memory_space=pltpu.SMEM)
    return pl.pallas_call(
        body,
        grid=(1,),
        out_shape=jax.ShapeDtypeStruct((64, TILE, TILE), BF16),
        in_specs=[smem, smem, pl.BlockSpec(child.shape, lambda i: (0, 0))],
        out_specs=pl.BlockSpec((64, TILE, TILE), lambda i: (0, 0, 0)),
        compiler_params=pltpu.CompilerParams(vmem_limit_bytes=14 << 20),
        cost_estimate=pl.CostEstimate(flops=0, bytes_accessed=4 << 20, transcendentals=0),
        name="pack_first",
    )(place, maps, child)


def pack_second(index, tiles):
    def body(index_ref, tiles_ref, out_ref):
        for slot in range(64):
            out_ref[slot] = tiles_ref[index_ref[slot]]

    return pl.pallas_call(
        body,
        out_shape=jax.ShapeDtypeStruct((64, TILE, TILE), BF16),
        in_specs=[
            pl.BlockSpec(memory_space=pltpu.SMEM),
            pl.BlockSpec(memory_space=pltpu.VMEM),
        ],
        out_specs=pl.BlockSpec(memory_space=pltpu.VMEM),
        compiler_params=pltpu.CompilerParams(vmem_limit_bytes=10 << 20),
        name="pack_second",
    )(index, tiles)


def split_dot(left, right, dims):
    l_hi = left.astype(BF16)
    l_lo = (left - l_hi.astype(F32)).astype(BF16)
    r_hi = right.astype(BF16)
    r_lo = (right - r_hi.astype(F32)).astype(BF16)
    dot = functools.partial(
        lax.dot_general, dimension_numbers=(dims, ((), ())), preferred_element_type=F32
    )
    return dot(l_hi, r_hi) + (dot(l_hi, r_lo) + dot(l_lo, r_hi))


def inverse_factor(gathered):
    group = 16

    def body(piece_ref, w_ref, big, small):
        lane = lax.broadcasted_iota(jnp.int32, (group, TILE), 1)
        sub = lax.broadcasted_iota(jnp.int32, (group, TILE), 0)
        lane_all = lax.broadcasted_iota(jnp.int32, (TILE, TILE), 1)
        row_all = lax.broadcasted_iota(jnp.int32, (TILE, TILE), 0)
        for s in range(4):
            for piece in range(16):
                at = s * TILE + piece * 8
                for t in range(4):
                    row = (s * 4 + t) * 8
                    big[at : at + 8, t * TILE : (t + 1) * TILE] = piece_ref[piece, row : row + 8, :]

        for j in range(4):
            start = j * TILE
            stop = start + TILE
            small[...] = big[start:stop, start:stop]
            for b in range(TILE // group):
                lo = group * b
                panel = small[lo : lo + group, :]
                unit = jnp.where(lane == sub + lo, 1.0, 0.0)
                cols = [
                    jnp.broadcast_to(panel[:, lo + m : lo + m + 1], (group, TILE))
                    for m in range(group)
                ]
                for m in range(group):
                    inv = lax.rsqrt(jnp.broadcast_to(cols[m][m : m + 1], (group, TILE)))
                    low = cols[m] * inv
                    for n in range(m + 1, group):
                        cols[n] = cols[n] - low * (
                            jnp.broadcast_to(cols[n][m : m + 1], (group, TILE)) * inv
                        )
                    low = jnp.where(sub > m, low, 0.0)
                    keep = jnp.where(sub == m, inv, 1.0)
                    panel = panel * keep - low * (
                        jnp.broadcast_to(panel[m : m + 1], (group, TILE)) * inv
                    )
                    unit = unit * keep - low * (
                        jnp.broadcast_to(unit[m : m + 1], (group, TILE)) * inv
                    )
                here = (lane >= lo) & (lane < lo + group)
                final = jnp.where(here, unit, panel)
                small[lo : lo + group, :] = final
                if lo + group < TILE:
                    p_hi = panel.astype(BF16).astype(F32)
                    f_hi = final.astype(BF16).astype(F32)
                    left = jnp.concatenate([p_hi, p_hi, panel - p_hi], axis=0).astype(BF16)
                    right = jnp.concatenate([f_hi, final - f_hi, f_hi], axis=0).astype(BF16)
                    change = lax.dot_general(
                        left, right, (((0,), (0,)), ((), ())), preferred_element_type=F32
                    )
                    rest = small[lo + group :, :]
                    in_block = lane_all[lo + group :, :]
                    in_block = (in_block >= lo) & (in_block < lo + group)
                    small[lo + group :, :] = jnp.where(in_block, 0.0, rest) - change[lo + group :, :]
            diag = jnp.where(row_all >= lane_all, small[...], 0.0)
            if j > 0:
                left_part = split_dot(diag, big[start:stop, :start], ((1,), (0,)))
                big[start:stop, :start] = left_part
            if j < 3:
                upper = split_dot(diag, big[start:stop, stop:], ((1,), (0,)))
                if j > 0:
                    big[stop:, :start] -= split_dot(upper, left_part, ((0,), (0,)))
                big[stop:, start:stop] = -split_dot(upper, diag, ((0,), (0,)))
                big[stop:, stop:] -= split_dot(upper, upper, ((0,), (0,)))
                big[start:stop, stop:] = jnp.zeros((TILE, KDIM - stop), F32)
            big[start:stop, start:stop] = diag
        w_ref[...] = big[...]

    return pl.pallas_call(
        body,
        grid=(1,),
        out_shape=jax.ShapeDtypeStruct((KDIM, KDIM), F32),
        in_specs=[pl.BlockSpec((16, TILE, TILE), lambda i: (0, 0, 0))],
        out_specs=pl.BlockSpec((KDIM, KDIM), lambda i: (0, 0)),
        scratch_shapes=[
            pltpu.VMEM((KDIM, KDIM), F32),
            pltpu.VMEM((TILE, TILE), F32),
        ],
        compiler_params=pltpu.CompilerParams(vmem_limit_bytes=16 << 20),
        name="inverse_factor",
    )(gathered)


def solve_rows(first_tile, gathered, inverse):
    def body(tile_ref, piece_ref, w_ref, g_ref, hi_ref, lo_ref, rows, w_hi, w_lo):
        lt = pl.program_id(0)

        @pl.when(lt == 0)
        def _():
            hi = w_ref[...].astype(BF16)
            w_hi[...] = hi
            w_lo[...] = (w_ref[...] - hi.astype(F32)).astype(BF16)

        for piece in range(16):
            for s in range(4):
                rows[piece * 8 : piece * 8 + 8, s * TILE : (s + 1) * TILE] = piece_ref[
                    piece, s * 8 : s * 8 + 8, :
                ]
        f_hi = rows[...].astype(BF16)
        f_lo = (rows[...] - f_hi.astype(F32)).astype(BF16)
        dot = functools.partial(
            lax.dot_general,
            dimension_numbers=(((1,), (1,)), ((), ())),
            preferred_element_type=F32,
        )
        g = dot(f_hi, w_hi[...]) + (dot(f_hi, w_lo[...]) + dot(f_lo, w_hi[...]))
        tile_no = tile_ref[0] + 8 * lt
        panel_no = lax.broadcasted_iota(jnp.int32, (TILE, KDIM), 1) // PANEL
        g = jnp.where(tile_no >= 2 * panel_no, g, 0.0)
        g_ref[...] = g
        h = jnp.where(tile_no >= 2 * panel_no + 2, g, 0.0)
        h_hi = h.astype(BF16)
        hi_ref[...] = h_hi
        lo_ref[...] = (h - h_hi.astype(F32)).astype(BF16)

    rows_spec = pl.BlockSpec((TILE, KDIM), lambda lt, tile: (lt, 0))
    return pl.pallas_call(
        body,
        grid_spec=pltpu.PrefetchScalarGridSpec(
            num_scalar_prefetch=1,
            grid=(12,),
            in_specs=[
                pl.BlockSpec((16, 32, TILE), lambda lt, tile: (0, lt, 0)),
                pl.BlockSpec((KDIM, KDIM), lambda lt, tile: (0, 0)),
            ],
            out_specs=[rows_spec, rows_spec, rows_spec],
            scratch_shapes=[
                pltpu.VMEM((TILE, KDIM), F32),
                pltpu.VMEM((KDIM, KDIM), BF16),
                pltpu.VMEM((KDIM, KDIM), BF16),
            ],
        ),
        out_shape=[
            jax.ShapeDtypeStruct((12 * TILE, KDIM), F32),
            jax.ShapeDtypeStruct((12 * TILE, KDIM), BF16),
            jax.ShapeDtypeStruct((12 * TILE, KDIM), BF16),
        ],
        compiler_params=pltpu.CompilerParams(vmem_limit_bytes=10 << 20),
        name="solve_rows",
    )(first_tile, gathered, inverse)


def trailing_update(front, rows_hi, rows_lo, trail):
    def body(front_ref, hi_ref, lo_ref, trail_ref, out_ref, cols):
        @pl.when(pl.program_id(0) == 0)
        def _():
            for j in range(6):
                for p in range(0, 8, 2):
                    one = trail_ref[p, 16 * j : 16 * j + 16, :].astype(F32)
                    two = trail_ref[p + 1, 16 * j : 16 * j + 16, :].astype(F32)
                    for h in range(2):
                        at = j * TILE + 64 * h + 8 * p
                        both = jnp.concatenate(
                            [one[8 * h : 8 * h + 8], two[8 * h : 8 * h + 8]], axis=0
                        )
                        cols[at : at + 16, :] = both.astype(BF16)

        dot = functools.partial(
            lax.dot_general,
            dimension_numbers=(((1,), (1,)), ((), ())),
            preferred_element_type=F32,
        )
        out_ref[...] = front_ref[...].astype(F32) - (
            dot(hi_ref[...], cols[...]) + dot(lo_ref[...], cols[...])
        )

    width = front.shape[1]
    return pl.pallas_call(
        body,
        grid=(6,),
        in_specs=[
            pl.BlockSpec((2 * TILE, width), lambda n: (n, 0)),
            pl.BlockSpec((2 * TILE, KDIM), lambda n: (n, 0)),
            pl.BlockSpec((2 * TILE, KDIM), lambda n: (n, 0)),
            pl.BlockSpec((8, 96, KDIM), lambda n: (0, 0, 0)),
        ],
        out_specs=pl.BlockSpec((2 * TILE, width), lambda n: (n, 0)),
        scratch_shapes=[pltpu.VMEM((6 * TILE, KDIM), BF16)],
        out_shape=jax.ShapeDtypeStruct(front.shape, F32),
        compiler_params=pltpu.CompilerParams(vmem_limit_bytes=56 << 20),
        name="trailing_update",
    )(front, rows_hi, rows_lo, trail)


def add_tiles(tile_at, col_at, base, tiles):
    per_step = 3

    def body(at_ref, col_ref, base_ref, tiles_ref, out_ref):
        out_ref[...] = base_ref[...]
        for m in range(per_step):
            for n in range(8):
                entry = (pl.program_id(0) * per_step + m) * 8 + n
                source = at_ref[entry]

                @pl.when(source >= 0)
                def _():
                    where_col = pl.multiple_of(col_ref[entry] * TILE, TILE)
                    out_ref[m * TILE : (m + 1) * TILE, pl.ds(where_col, TILE)] += tiles_ref[
                        source
                    ].astype(F32)

    block = (per_step * TILE, base.shape[1])
    return pl.pallas_call(
        body,
        grid_spec=pltpu.PrefetchScalarGridSpec(
            num_scalar_prefetch=2,
            grid=(12 // per_step,),
            in_specs=[
                pl.BlockSpec(block, lambda step, a, b: (step, 0)),
                pl.BlockSpec((64, TILE, TILE), lambda step, a, b: (0, 0, 0)),
            ],
            out_specs=pl.BlockSpec(block, lambda step, a, b: (step, 0)),
        ),
        out_shape=jax.ShapeDtypeStruct(base.shape, F32),
        input_output_aliases={2: 0},
        compiler_params=pltpu.CompilerParams(vmem_limit_bytes=14 << 20),
        name="add_tiles",
    )(tile_at, col_at, base, tiles)


def per_device(front_orig, child_update, tile_map):
    fr = lax.axis_index("front")
    r = lax.axis_index(ROW)
    c = lax.axis_index(COL)
    xlo = r % 2
    child_no = c // 4
    quarter = c % 4
    maps = tile_map.reshape(4, NCT)
    front = front_orig[0]

    place = jnp.stack([child_no, quarter]).astype(jnp.int32)
    message = pack_panel(place, maps, child_update, front)
    first_tiles = pack_first(place, maps, child_update)
    got = lax.all_to_all(message, COL, split_axis=0, concat_axis=0, tiled=True)
    child_piece = got[:, :128].reshape(4, 4, 128, TILE).astype(F32).sum(axis=1).astype(BF16)
    front_piece = got[:4, 128:].reshape(4, 12, PIECE, TILE)
    diag_piece = front_piece[:, 0].reshape(4 * PIECE, TILE)
    to_front = jnp.concatenate(
        [child_piece.reshape(2, 256, TILE), jnp.broadcast_to(diag_piece, (2, 32, TILE))], axis=1
    )
    message = jnp.broadcast_to(to_front[:, None], (2, 8, 288, TILE)).reshape(16, 288, TILE)
    got = lax.all_to_all(message, ("front",) + ROW, split_axis=0, concat_axis=0, tiled=True)
    blocks = got[:, :256].reshape(16, 2, 4, 4, PIECE, TILE)
    own_maps = lax.dynamic_slice(maps, (2 * fr, 0), (2, NCT))
    wanted = jnp.concatenate([r + 8 * jnp.arange(12), jnp.arange(4)])
    one_hot = (own_maps.reshape(1, 2, 16, 4) == wanted[:, None, None, None]).astype(BF16)
    added = jnp.einsum("tkna,nksapl->tspl", one_hot, blocks, preferred_element_type=F32)
    diag_front = lax.dynamic_slice(got, (8 * fr, 256, 0), (4, 32, TILE))
    front_part = jnp.concatenate(
        [front_piece.transpose(1, 0, 2, 3), diag_front.reshape(4, 4, PIECE, TILE)], axis=0
    )
    chunk = added + front_part.astype(F32)
    diag_all = lax.all_gather(chunk[12:].reshape(128, TILE), COL, axis=0)
    panel_all = lax.all_gather(chunk[:12].reshape(384, TILE), COL, axis=0)
    inverse = inverse_factor(diag_all)

    panel_chunk = chunk[:12].transpose(0, 2, 1, 3).reshape(12 * PIECE, KDIM)
    g_chunk = lax.dot_general(
        panel_chunk,
        inverse,
        (((1,), (1,)), ((), ())),
        precision=lax.Precision.HIGHEST,
        preferred_element_type=F32,
    )
    chunk_t = jnp.repeat(r + 8 * jnp.arange(12), PIECE)[:, None]
    after = 2 * (jnp.arange(KDIM)[None, :] // PANEL) + 2
    h_chunk = jnp.where(chunk_t >= after, g_chunk, 0.0).astype(BF16)
    h_chunk = h_chunk.reshape(6, 2, PIECE, KDIM).transpose(1, 0, 2, 3)
    h_own = c // 8
    same = lax.dynamic_index_in_dim(h_chunk, h_own, 0, keepdims=False)
    cross = lax.dynamic_index_in_dim(h_chunk, 1 - h_own, 0, keepdims=False)
    route_same, route_cross = [], []
    for rr in range(8):
        for cc in range(16):
            h, m = cc // 8, cc % 8
            route_same.append((rr * 16 + cc, m * 16 + 8 * h + rr))
            route_cross.append((rr * 16 + cc, m * 16 + 8 * (1 - h) + rr))
    same = lax.ppermute(same, ROW + COL, route_same)
    cross = lax.ppermute(cross, ROW + COL, route_cross)
    first = jnp.where(h_own == 0, same, cross)
    second = jnp.where(h_own == 0, cross, same)
    piece = jnp.concatenate([first, second], axis=1).reshape(96, KDIM)
    trail = lax.all_to_all(
        jnp.broadcast_to(piece, (8, 96, KDIM)), ROW, split_axis=0, concat_axis=0, tiled=True
    )

    message = first_tiles.reshape(32, 2 * TILE, TILE)
    got = lax.all_to_all(message, ("xlo",) + COL, split_axis=0, concat_axis=0, tiled=True)
    got, trail = lax.optimization_barrier((got, trail))
    class_of = jnp.argmax(
        (maps[:, None, :8] % 8) == jnp.arange(8)[None, :, None], axis=2
    ).astype(jnp.int32)
    kid = jnp.arange(4).reshape(2, 1, 2, 1)
    dest_row = jnp.arange(8).reshape(1, 8, 1, 1)
    half = jnp.arange(2).reshape(1, 1, 1, 2)
    klass = class_of[kid, dest_row]
    q_no = 2 * half + (((klass % 4) // 2) ^ xlo)
    source = ((klass // 4) * 16 + 4 * kid + q_no) * 2 + (klass & 1)
    message = pack_second(source.reshape(64).astype(jnp.int32), got.reshape(64, TILE, TILE))
    message = message.reshape(16, 4 * TILE, TILE)
    got = lax.all_to_all(message, ("front",) + ROW, split_axis=0, concat_axis=0, tiled=True)
    tiles = got.reshape(64, TILE, TILE)
    match = own_maps[None] == (r + 8 * jnp.arange(12))[:, None, None]
    i_no = jnp.argmax(match, axis=2).astype(jnp.int32)[:, :, None, None]
    present = jnp.any(match, axis=2)[:, :, None, None]
    sib = jnp.arange(2).reshape(1, 2, 1, 1)
    x_from = jnp.arange(2).reshape(1, 1, 2, 1)
    half = jnp.arange(2).reshape(1, 1, 1, 2)
    sender = (i_no // 32) * 8 + (i_no % 32) // 8 * 2 + x_from
    tile_at = jnp.where(present, (sender * 2 + sib) * 2 + half, -1)
    col_b = jnp.argmax((own_maps[:, :16] % 16) == c, axis=1).astype(jnp.int32)
    col_tiles = own_maps.reshape(2, 4, 16)
    col_tiles = jnp.take_along_axis(col_tiles, col_b.reshape(2, 1, 1), axis=2)[:, :, 0] // 16
    q_no = 2 * half + (((i_no % 4) // 2) ^ x_from)
    col_at = jnp.zeros(q_no.shape[:1] + (2, 2, 2), jnp.int32)
    for q in range(4):
        col_at = jnp.where(q_no == q, col_tiles[:, q].reshape(1, 2, 1, 1), col_at)

    factor, rows_hi, rows_lo = solve_rows(r.reshape(1).astype(jnp.int32), panel_all, inverse)
    base = trailing_update(front, rows_hi, rows_lo, trail)
    update = add_tiles(
        tile_at.reshape(96).astype(jnp.int32), col_at.reshape(96).astype(jnp.int32), base, tiles
    )
    return (update[None], factor[None])


def solution(mesh):
    fine = Mesh(
        mesh.devices.reshape(2, 4, 2, 8, 2), ("front", "rowh", "xlo", "z", "core")
    )
    return jax.shard_map(
        per_device,
        mesh=fine,
        in_specs=(P("front", ROW, COL), P(("front",) + ROW, COL), P()),
        out_specs=(P("front", ROW, COL), P("front", ROW, None)),
        check_vma=False,
    )
```

```python
import functools

import jax
import jax.numpy as jnp
from jax import lax
from jax.experimental import pallas as pl
from jax.experimental.pallas import tpu as pltpu
from jax.sharding import Mesh
from jax.sharding import PartitionSpec as P

TILE = 128
PANEL = 256
KDIM = 512
NT = 96
NCT = 64
ROW = ("rowh", "xlo")
COL = ("z", "core")
PIECE = 8
F32 = jnp.float32
BF16 = jnp.bfloat16


def pack_panel(place, maps, child, front):
    def locate(s, place_ref, maps_ref):
        found = jnp.int32(-1)
        for b in range(16):
            target = maps_ref[place_ref[0], 16 * place_ref[1] + b]
            found = jnp.where(target == s, b, found)
        return found

    def body(place_ref, maps_ref, *refs):
        strips, front_ref, panel_ref = refs[:4], refs[4], refs[5]

        def spread(block, at, count):
            for c in range(16):
                for n in range(0, count, 2):
                    pair = [block[m * TILE + 8 * c : m * TILE + 8 * c + 8] for m in (n, n + 1)]
                    panel_ref[c, at + 8 * n : at + 8 * n + 16, :] = jnp.concatenate(
                        pair, axis=0
                    ).astype(BF16)

        for s in range(4):
            strip = strips[s][...].astype(F32)
            spread(jnp.where(locate(s, place_ref, maps_ref) >= 0, strip, 0.0), 32 * s, 4)
        spread(front_ref[...].astype(F32), 128, 12)

    def strip_spec(s):
        return pl.BlockSpec(
            (4 * TILE, TILE), lambda i, p, m: (0, jnp.maximum(locate(s, p, m), 0))
        )

    return pl.pallas_call(
        body,
        grid_spec=pltpu.PrefetchScalarGridSpec(
            num_scalar_prefetch=2,
            grid=(1,),
            in_specs=[strip_spec(s) for s in range(4)]
            + [pl.BlockSpec((12 * TILE, TILE), lambda i, p, m: (0, 0))],
            out_specs=pl.BlockSpec((16, 224, TILE), lambda i, p, m: (0, 0, 0)),
        ),
        out_shape=jax.ShapeDtypeStruct((16, 224, TILE), BF16),
        compiler_params=pltpu.CompilerParams(vmem_limit_bytes=56 << 20),
        name="pack_panel",
    )(place, maps, child, child, child, child, front)


def pack_first(place, maps, child):
    def body(place_ref, maps_ref, child_ref, tiles_ref):
        child_no, quarter = place_ref[0], place_ref[1]
        for b in range(16):
            col = maps_ref[child_no, 16 * quarter + b] % 16
            for a in range(4):
                to = ((a // 2) ^ (quarter % 2)) * 32 + col * 2 + a % 2
                tile = child_ref[a * TILE : (a + 1) * TILE, b * TILE : (b + 1) * TILE]
                tiles_ref[to] = tile

    smem = pl.BlockSpec(memory_space=pltpu.SMEM)
    return pl.pallas_call(
        body,
        grid=(1,),
        out_shape=jax.ShapeDtypeStruct((64, TILE, TILE), BF16),
        in_specs=[smem, smem, pl.BlockSpec(child.shape, lambda i: (0, 0))],
        out_specs=pl.BlockSpec((64, TILE, TILE), lambda i: (0, 0, 0)),
        compiler_params=pltpu.CompilerParams(vmem_limit_bytes=14 << 20),
        cost_estimate=pl.CostEstimate(flops=0, bytes_accessed=4 << 20, transcendentals=0),
        name="pack_first",
    )(place, maps, child)


def pack_second(index, tiles):
    def body(index_ref, tiles_ref, out_ref):
        for slot in range(64):
            out_ref[slot] = tiles_ref[index_ref[slot]]

    return pl.pallas_call(
        body,
        out_shape=jax.ShapeDtypeStruct((64, TILE, TILE), BF16),
        in_specs=[
            pl.BlockSpec(memory_space=pltpu.SMEM),
            pl.BlockSpec(memory_space=pltpu.VMEM),
        ],
        out_specs=pl.BlockSpec(memory_space=pltpu.VMEM),
        compiler_params=pltpu.CompilerParams(vmem_limit_bytes=10 << 20),
        name="pack_second",
    )(index, tiles)


def split_dot(left, right, dims):
    l_hi = left.astype(BF16)
    l_lo = (left - l_hi.astype(F32)).astype(BF16)
    r_hi = right.astype(BF16)
    r_lo = (right - r_hi.astype(F32)).astype(BF16)
    dot = functools.partial(
        lax.dot_general, dimension_numbers=(dims, ((), ())), preferred_element_type=F32
    )
    return dot(l_hi, r_hi) + (dot(l_hi, r_lo) + dot(l_lo, r_hi))


def inverse_factor(gathered):
    group = 16

    def body(piece_ref, w_ref, big, small):
        lane = lax.broadcasted_iota(jnp.int32, (group, TILE), 1)
        sub = lax.broadcasted_iota(jnp.int32, (group, TILE), 0)
        lane_all = lax.broadcasted_iota(jnp.int32, (TILE, TILE), 1)
        row_all = lax.broadcasted_iota(jnp.int32, (TILE, TILE), 0)
        for s in range(4):
            for piece in range(16):
                at = s * TILE + piece * 8
                for t in range(4):
                    row = (s * 4 + t) * 8
                    big[at : at + 8, t * TILE : (t + 1) * TILE] = piece_ref[piece, row : row + 8, :]

        for j in range(4):
            start = j * TILE
            stop = start + TILE
            small[...] = big[start:stop, start:stop]
            for b in range(TILE // group):
                lo = group * b
                panel = small[lo : lo + group, :]
                unit = jnp.where(lane == sub + lo, 1.0, 0.0)
                cols = [
                    jnp.broadcast_to(panel[:, lo + m : lo + m + 1], (group, TILE))
                    for m in range(group)
                ]
                for m in range(group):
                    inv = lax.rsqrt(jnp.broadcast_to(cols[m][m : m + 1], (group, TILE)))
                    low = cols[m] * inv
                    for n in range(m + 1, group):
                        cols[n] = cols[n] - low * (
                            jnp.broadcast_to(cols[n][m : m + 1], (group, TILE)) * inv
                        )
                    low = jnp.where(sub > m, low, 0.0)
                    keep = jnp.where(sub == m, inv, 1.0)
                    panel = panel * keep - low * (
                        jnp.broadcast_to(panel[m : m + 1], (group, TILE)) * inv
                    )
                    unit = unit * keep - low * (
                        jnp.broadcast_to(unit[m : m + 1], (group, TILE)) * inv
                    )
                here = (lane >= lo) & (lane < lo + group)
                final = jnp.where(here, unit, panel)
                small[lo : lo + group, :] = final
                if lo + group < TILE:
                    p_hi = panel.astype(BF16).astype(F32)
                    f_hi = final.astype(BF16).astype(F32)
                    left = jnp.concatenate([p_hi, p_hi, panel - p_hi], axis=0).astype(BF16)
                    right = jnp.concatenate([f_hi, final - f_hi, f_hi], axis=0).astype(BF16)
                    change = lax.dot_general(
                        left, right, (((0,), (0,)), ((), ())), preferred_element_type=F32
                    )
                    rest = small[lo + group :, :]
                    in_block = lane_all[lo + group :, :]
                    in_block = (in_block >= lo) & (in_block < lo + group)
                    small[lo + group :, :] = jnp.where(in_block, 0.0, rest) - change[lo + group :, :]
            diag = jnp.where(row_all >= lane_all, small[...], 0.0)
            if j > 0:
                left_part = split_dot(diag, big[start:stop, :start], ((1,), (0,)))
                big[start:stop, :start] = left_part
            if j < 3:
                upper = split_dot(diag, big[start:stop, stop:], ((1,), (0,)))
                if j > 0:
                    big[stop:, :start] -= split_dot(upper, left_part, ((0,), (0,)))
                big[stop:, start:stop] = -split_dot(upper, diag, ((0,), (0,)))
                big[stop:, stop:] -= split_dot(upper, upper, ((0,), (0,)))
                big[start:stop, stop:] = jnp.zeros((TILE, KDIM - stop), F32)
            big[start:stop, start:stop] = diag
        w_ref[...] = big[...]

    return pl.pallas_call(
        body,
        grid=(1,),
        out_shape=jax.ShapeDtypeStruct((KDIM, KDIM), F32),
        in_specs=[pl.BlockSpec((16, TILE, TILE), lambda i: (0, 0, 0))],
        out_specs=pl.BlockSpec((KDIM, KDIM), lambda i: (0, 0)),
        scratch_shapes=[
            pltpu.VMEM((KDIM, KDIM), F32),
            pltpu.VMEM((TILE, TILE), F32),
        ],
        compiler_params=pltpu.CompilerParams(vmem_limit_bytes=16 << 20),
        name="inverse_factor",
    )(gathered)


def solve_rows(first_tile, gathered, inverse):
    def body(tile_ref, piece_ref, w_ref, g_ref, hi_ref, lo_ref, rows, w_hi, w_lo):
        lt = pl.program_id(0)

        @pl.when(lt == 0)
        def _():
            hi = w_ref[...].astype(BF16)
            w_hi[...] = hi
            w_lo[...] = (w_ref[...] - hi.astype(F32)).astype(BF16)

        for piece in range(16):
            for s in range(4):
                rows[piece * 8 : piece * 8 + 8, s * TILE : (s + 1) * TILE] = piece_ref[
                    piece, s * 8 : s * 8 + 8, :
                ]
        f_hi = rows[...].astype(BF16)
        f_lo = (rows[...] - f_hi.astype(F32)).astype(BF16)
        dot = functools.partial(
            lax.dot_general,
            dimension_numbers=(((1,), (1,)), ((), ())),
            preferred_element_type=F32,
        )
        g = dot(f_hi, w_hi[...]) + (dot(f_hi, w_lo[...]) + dot(f_lo, w_hi[...]))
        tile_no = tile_ref[0] + 8 * lt
        panel_no = lax.broadcasted_iota(jnp.int32, (TILE, KDIM), 1) // PANEL
        g = jnp.where(tile_no >= 2 * panel_no, g, 0.0)
        g_ref[...] = g
        h = jnp.where(tile_no >= 2 * panel_no + 2, g, 0.0)
        h_hi = h.astype(BF16)
        hi_ref[...] = h_hi
        lo_ref[...] = (h - h_hi.astype(F32)).astype(BF16)

    rows_spec = pl.BlockSpec((TILE, KDIM), lambda lt, tile: (lt, 0))
    return pl.pallas_call(
        body,
        grid_spec=pltpu.PrefetchScalarGridSpec(
            num_scalar_prefetch=1,
            grid=(12,),
            in_specs=[
                pl.BlockSpec((16, 32, TILE), lambda lt, tile: (0, lt, 0)),
                pl.BlockSpec((KDIM, KDIM), lambda lt, tile: (0, 0)),
            ],
            out_specs=[rows_spec, rows_spec, rows_spec],
            scratch_shapes=[
                pltpu.VMEM((TILE, KDIM), F32),
                pltpu.VMEM((KDIM, KDIM), BF16),
                pltpu.VMEM((KDIM, KDIM), BF16),
            ],
        ),
        out_shape=[
            jax.ShapeDtypeStruct((12 * TILE, KDIM), F32),
            jax.ShapeDtypeStruct((12 * TILE, KDIM), BF16),
            jax.ShapeDtypeStruct((12 * TILE, KDIM), BF16),
        ],
        compiler_params=pltpu.CompilerParams(vmem_limit_bytes=10 << 20),
        name="solve_rows",
    )(first_tile, gathered, inverse)


def trailing_update(front, rows_hi, rows_lo, trail):
    def body(front_ref, hi_ref, lo_ref, trail_ref, out_ref, cols):
        @pl.when(pl.program_id(0) == 0)
        def _():
            for j in range(6):
                for p in range(0, 8, 2):
                    one = trail_ref[p, 16 * j : 16 * j + 16, :].astype(F32)
                    two = trail_ref[p + 1, 16 * j : 16 * j + 16, :].astype(F32)
                    for h in range(2):
                        at = j * TILE + 64 * h + 8 * p
                        both = jnp.concatenate(
                            [one[8 * h : 8 * h + 8], two[8 * h : 8 * h + 8]], axis=0
                        )
                        cols[at : at + 16, :] = both.astype(BF16)

        dot = functools.partial(
            lax.dot_general,
            dimension_numbers=(((1,), (1,)), ((), ())),
            preferred_element_type=F32,
        )
        out_ref[...] = front_ref[...].astype(F32) - (
            dot(hi_ref[...], cols[...]) + dot(lo_ref[...], cols[...])
        )

    width = front.shape[1]
    return pl.pallas_call(
        body,
        grid=(6,),
        in_specs=[
            pl.BlockSpec((2 * TILE, width), lambda n: (n, 0)),
            pl.BlockSpec((2 * TILE, KDIM), lambda n: (n, 0)),
            pl.BlockSpec((2 * TILE, KDIM), lambda n: (n, 0)),
            pl.BlockSpec((8, 96, KDIM), lambda n: (0, 0, 0)),
        ],
        out_specs=pl.BlockSpec((2 * TILE, width), lambda n: (n, 0)),
        scratch_shapes=[pltpu.VMEM((6 * TILE, KDIM), BF16)],
        out_shape=jax.ShapeDtypeStruct(front.shape, F32),
        compiler_params=pltpu.CompilerParams(vmem_limit_bytes=56 << 20),
        name="trailing_update",
    )(front, rows_hi, rows_lo, trail)


def add_tiles(tile_at, col_at, base, tiles):
    per_step = 3

    def body(at_ref, col_ref, base_ref, tiles_ref, out_ref):
        out_ref[...] = base_ref[...]
        for m in range(per_step):
            for n in range(8):
                entry = (pl.program_id(0) * per_step + m) * 8 + n
                source = at_ref[entry]

                @pl.when(source >= 0)
                def _():
                    where_col = pl.multiple_of(col_ref[entry] * TILE, TILE)
                    out_ref[m * TILE : (m + 1) * TILE, pl.ds(where_col, TILE)] += tiles_ref[
                        source
                    ].astype(F32)

    block = (per_step * TILE, base.shape[1])
    return pl.pallas_call(
        body,
        grid_spec=pltpu.PrefetchScalarGridSpec(
            num_scalar_prefetch=2,
            grid=(12 // per_step,),
            in_specs=[
                pl.BlockSpec(block, lambda step, a, b: (step, 0)),
                pl.BlockSpec((64, TILE, TILE), lambda step, a, b: (0, 0, 0)),
            ],
            out_specs=pl.BlockSpec(block, lambda step, a, b: (step, 0)),
        ),
        out_shape=jax.ShapeDtypeStruct(base.shape, F32),
        input_output_aliases={2: 0},
        compiler_params=pltpu.CompilerParams(vmem_limit_bytes=14 << 20),
        name="add_tiles",
    )(tile_at, col_at, base, tiles)


def per_device(front_orig, child_update, tile_map):
    fr = lax.axis_index("front")
    r = lax.axis_index(ROW)
    c = lax.axis_index(COL)
    xlo = r % 2
    child_no = c // 4
    quarter = c % 4
    maps = tile_map.reshape(4, NCT)
    front = front_orig[0]

    place = jnp.stack([child_no, quarter]).astype(jnp.int32)
    message = pack_panel(place, maps, child_update, front)
    first_tiles = pack_first(place, maps, child_update)
    got = lax.all_to_all(message, COL, split_axis=0, concat_axis=0, tiled=True)
    child_piece = got[:, :128].reshape(4, 4, 128, TILE).astype(F32).sum(axis=1).astype(BF16)
    front_piece = got[:4, 128:].reshape(4, 12, PIECE, TILE)
    diag_piece = front_piece[:, 0].reshape(4 * PIECE, TILE)
    to_front = jnp.concatenate(
        [child_piece.reshape(2, 256, TILE), jnp.broadcast_to(diag_piece, (2, 32, TILE))], axis=1
    )
    message = jnp.broadcast_to(to_front[:, None], (2, 8, 288, TILE)).reshape(16, 288, TILE)
    got = lax.all_to_all(message, ("front",) + ROW, split_axis=0, concat_axis=0, tiled=True)
    blocks = got[:, :256].reshape(16, 2, 4, 4, PIECE, TILE)
    own_maps = lax.dynamic_slice(maps, (2 * fr, 0), (2, NCT))
    wanted = jnp.concatenate([r + 8 * jnp.arange(12), jnp.arange(4)])
    one_hot = (own_maps.reshape(1, 2, 16, 4) == wanted[:, None, None, None]).astype(BF16)
    added = jnp.einsum("tkna,nksapl->tspl", one_hot, blocks, preferred_element_type=F32)
    diag_front = lax.dynamic_slice(got, (8 * fr, 256, 0), (4, 32, TILE))
    front_part = jnp.concatenate(
        [front_piece.transpose(1, 0, 2, 3), diag_front.reshape(4, 4, PIECE, TILE)], axis=0
    )
    chunk = added + front_part.astype(F32)
    chunk, first_tiles = lax.optimization_barrier((chunk, first_tiles))
    diag_all = lax.all_gather(chunk[12:].reshape(128, TILE), COL, axis=0)
    panel_all = lax.all_gather(chunk[:12].reshape(384, TILE), COL, axis=0)
    inverse = inverse_factor(diag_all)

    panel_chunk = chunk[:12].transpose(0, 2, 1, 3).reshape(12 * PIECE, KDIM)
    g_chunk = lax.dot_general(
        panel_chunk,
        inverse,
        (((1,), (1,)), ((), ())),
        precision=lax.Precision.HIGHEST,
        preferred_element_type=F32,
    )
    chunk_t = jnp.repeat(r + 8 * jnp.arange(12), PIECE)[:, None]
    after = 2 * (jnp.arange(KDIM)[None, :] // PANEL) + 2
    h_chunk = jnp.where(chunk_t >= after, g_chunk, 0.0).astype(BF16)
    h_chunk = h_chunk.reshape(6, 2, PIECE, KDIM).transpose(1, 0, 2, 3)
    h_own = c // 8
    same = lax.dynamic_index_in_dim(h_chunk, h_own, 0, keepdims=False)
    cross = lax.dynamic_index_in_dim(h_chunk, 1 - h_own, 0, keepdims=False)
    route_same, route_cross = [], []
    for rr in range(8):
        for cc in range(16):
            h, m = cc // 8, cc % 8
            route_same.append((rr * 16 + cc, m * 16 + 8 * h + rr))
            route_cross.append((rr * 16 + cc, m * 16 + 8 * (1 - h) + rr))
    same = lax.ppermute(same, ROW + COL, route_same)
    cross = lax.ppermute(cross, ROW + COL, route_cross)
    first = jnp.where(h_own == 0, same, cross)
    second = jnp.where(h_own == 0, cross, same)
    piece = jnp.concatenate([first, second], axis=1).reshape(96, KDIM)
    message = first_tiles.reshape(32, 2 * TILE, TILE)
    got = lax.all_to_all(message, ("xlo",) + COL, split_axis=0, concat_axis=0, tiled=True)
    got, piece = lax.optimization_barrier((got, piece))
    trail = lax.all_to_all(
        jnp.broadcast_to(piece, (8, 96, KDIM)), ROW, split_axis=0, concat_axis=0, tiled=True
    )
    got, trail = lax.optimization_barrier((got, trail))
    class_of = jnp.argmax(
        (maps[:, None, :8] % 8) == jnp.arange(8)[None, :, None], axis=2
    ).astype(jnp.int32)
    kid = jnp.arange(4).reshape(2, 1, 2, 1)
    dest_row = jnp.arange(8).reshape(1, 8, 1, 1)
    half = jnp.arange(2).reshape(1, 1, 1, 2)
    klass = class_of[kid, dest_row]
    q_no = 2 * half + (((klass % 4) // 2) ^ xlo)
    source = ((klass // 4) * 16 + 4 * kid + q_no) * 2 + (klass & 1)
    message = pack_second(source.reshape(64).astype(jnp.int32), got.reshape(64, TILE, TILE))
    message = message.reshape(16, 4 * TILE, TILE)
    got = lax.all_to_all(message, ("front",) + ROW, split_axis=0, concat_axis=0, tiled=True)
    tiles = got.reshape(64, TILE, TILE)
    match = own_maps[None] == (r + 8 * jnp.arange(12))[:, None, None]
    i_no = jnp.argmax(match, axis=2).astype(jnp.int32)[:, :, None, None]
    present = jnp.any(match, axis=2)[:, :, None, None]
    sib = jnp.arange(2).reshape(1, 2, 1, 1)
    x_from = jnp.arange(2).reshape(1, 1, 2, 1)
    half = jnp.arange(2).reshape(1, 1, 1, 2)
    sender = (i_no // 32) * 8 + (i_no % 32) // 8 * 2 + x_from
    tile_at = jnp.where(present, (sender * 2 + sib) * 2 + half, -1)
    col_b = jnp.argmax((own_maps[:, :16] % 16) == c, axis=1).astype(jnp.int32)
    col_tiles = own_maps.reshape(2, 4, 16)
    col_tiles = jnp.take_along_axis(col_tiles, col_b.reshape(2, 1, 1), axis=2)[:, :, 0] // 16
    q_no = 2 * half + (((i_no % 4) // 2) ^ x_from)
    col_at = jnp.zeros(q_no.shape[:1] + (2, 2, 2), jnp.int32)
    for q in range(4):
        col_at = jnp.where(q_no == q, col_tiles[:, q].reshape(1, 2, 1, 1), col_at)

    factor, rows_hi, rows_lo = solve_rows(r.reshape(1).astype(jnp.int32), panel_all, inverse)
    base = trailing_update(front, rows_hi, rows_lo, trail)
    update = add_tiles(
        tile_at.reshape(96).astype(jnp.int32), col_at.reshape(96).astype(jnp.int32), base, tiles
    )
    return (update[None], factor[None])


def solution(mesh):
    fine = Mesh(
        mesh.devices.reshape(2, 4, 2, 8, 2), ("front", "rowh", "xlo", "z", "core")
    )
    return jax.shard_map(
        per_device,
        mesh=fine,
        in_specs=(P("front", ROW, COL), P(("front",) + ROW, COL), P()),
        out_specs=(P("front", ROW, COL), P("front", ROW, None)),
        check_vma=False,
    )
```
